128 devices in a mesh: section: 2 (over x_hi), req: 8 (over x_lo, y), tp: 8 (over z, core).
Axes of the slice: x: 4 (x_hi: 2, x_lo: 2; x = x_hi * 2 + x_lo), y: 4, z: 4, core: 2. Of those that a mesh axis runs over, the one named last changes fastest.
Arguments:
- stretch_query: bfloat16 [32768, 8192], P(('section', 'req'), 'tp'), may hold values from -16 to 16
- stretch_kv: bfloat16 [32768, 8, 256], P(('section', 'req'), 'tp'), may hold values from -16 to 16
- prefix_page_store: bfloat16 [1536, 64, 8, 256], P(('section', 'req'), None, 'tp'), may hold values from -6 to 6
- page_table: int32 [64, 24], P(('section', 'req')), may hold values from 0 to 95, as said below
- vs_mask: int32 [64, 64, 8, 32], P(('section', 'req'), 'tp'), may hold values from 0 to 1, as said below
- prompt_lengths: int32 [64], replicated, may hold values from 1 to 512, as said below
- placement: int32 [16, 4], replicated, may hold values from 0 to 7, as said below
- step_query_rows: bfloat16 [16, 8, 2, 8192], P(('section', 'req')), may hold values from -16 to 16
- step_key_value: bfloat16 [16, 8, 2, 8, 256], P(('section', 'req')), may hold values from -16 to 16
- selected_prefix_blocks: int32 [16, 8, 2, 64, 8], P(('section', 'req')), may hold values from 0 to 23, as said below
Outputs:
- prefill_out: bfloat16 [32768, 8192], P(('section', 'req'), 'tp')
- slot_page_store: bfloat16 [16, 8, 32, 64, 8, 256], P(('section', 'req'), None, 'tp')
- decode_output: bfloat16 [16, 8, 2, 8192], P(('section', 'req'))
The draws below stay inside these ranges and needn't reach their ends.
Inputs may be any that keep to these rules, and one draw needn't show every extreme that they name: `page_table`: within the 4 rows of one prefill group the entries are a permutation of 0 .. 95. `vs_mask`: block (a, b) is set only if b <= 24 + a; the diagonal block b = 24 + a is always set; every row a has at most 16 set blocks, and the last row has exactly 16. Prompt r has 1536 + prompt_lengths[r] tokens. `placement`: row s * 8 + g lists the decode groups, in section 1 - s, of the 4 prompts of prefill group g of section s; the entries of a row are distinct, and in each section some decode group receives a prompt from every prefill group of the other section. `selected_prefix_blocks`: the 8 entries of one slot, step and head are distinct.
All inputs are finite; a program needn't handle non-finite values.
Results may differ from the reference program's by a relative error of at most 0.0089.
Values may be sent and summed in bfloat16 or wider, within the bound.
No kernel may reach another device: no remote copies, remote signals or barrier semaphores. Data moves between devices by JAX's collectives and lax.ppermute only.
A program may use at most 192 MiB of HBM per device.

```python
import math
import jax
import jax.numpy as jnp
from jax import lax

QUERY_HEADS = 64
KEY_VALUE_HEADS = 8
HEAD_SIZE = 128
PRE = 1536
STRETCH_TOKENS = 512
BLOCK_TOKENS = 64
REQ_DEV = 4
DECODE_STEPS = 2
REQUEST_GROUPS = 16
PROMPT_COUNT = 64
DECODE_SLOTS = 8
NBP = 24
STRETCH_BLOCKS = 8
PROMPT_BLOCKS = 32
NV = 8
SELECTED_BLOCKS = 8
PREFIX_PAGES = 96
N_SECTION = 2
N_REQ = 8


def draw_stretch_query(key, part):
    key = jax.random.fold_in(key, 11)
    value_matrix = jnp.clip(jax.random.normal(key, (PROMPT_COUNT * STRETCH_TOKENS, QUERY_HEADS, HEAD_SIZE), jnp.float32), -6.0, 6.0)
    return value_matrix.reshape(PROMPT_COUNT * STRETCH_TOKENS, QUERY_HEADS * HEAD_SIZE).astype(jnp.bfloat16)


def draw_stretch_kv(key, part):
    key = jax.random.fold_in(key, 12)
    value_matrix = jnp.clip(jax.random.normal(key, (PROMPT_COUNT * STRETCH_TOKENS, KEY_VALUE_HEADS, 2 * HEAD_SIZE), jnp.float32), -6.0, 6.0)
    return value_matrix.astype(jnp.bfloat16)


def draw_step_query_rows(key, part):
    key = jax.random.fold_in(key, 13)
    slot_overall = REQUEST_GROUPS * DECODE_SLOTS
    value_matrix = jnp.clip(jax.random.normal(key, (slot_overall, DECODE_STEPS, QUERY_HEADS, HEAD_SIZE), jnp.float32), -6.0, 6.0)
    return value_matrix.reshape(REQUEST_GROUPS, DECODE_SLOTS, DECODE_STEPS, QUERY_HEADS * HEAD_SIZE).astype(jnp.bfloat16)


def draw_step_key_value(key, part):
    key = jax.random.fold_in(key, 14)
    slot_overall = REQUEST_GROUPS * DECODE_SLOTS
    value_matrix = jnp.clip(jax.random.normal(key, (slot_overall, DECODE_STEPS, KEY_VALUE_HEADS, 2 * HEAD_SIZE), jnp.float32), -6.0, 6.0)
    return value_matrix.reshape(REQUEST_GROUPS, DECODE_SLOTS, DECODE_STEPS, KEY_VALUE_HEADS, 2 * HEAD_SIZE).astype(jnp.bfloat16)


def vertical_slash(seed_key):
    vertical_key, slash_key = jax.random.split(seed_key)
    verticals = jax.random.permutation(vertical_key, NBP // 2)[:NV]
    slashes = jnp.concatenate([jnp.zeros((1,), jnp.int32), 1 + jax.random.permutation(slash_key, STRETCH_BLOCKS + NBP // 2 - 1)[:STRETCH_BLOCKS - 1].astype(jnp.int32)])
    query_block = jnp.arange(STRETCH_BLOCKS)[:, None]
    key_block = jnp.arange(PROMPT_BLOCKS)[None, :]
    diagonal = NBP + query_block
    vertical_hit = jnp.any(key_block[..., None] == verticals, axis=-1)
    slash_hit = jnp.any((diagonal - key_block)[..., None] == slashes, axis=-1)
    return ((key_block <= diagonal) & (vertical_hit | slash_hit)).astype(jnp.int32)


def draw_vs_mask(key, part):
    key = jax.random.fold_in(key, 21)
    subkeys = jax.random.split(key, PROMPT_COUNT * QUERY_HEADS)
    patterns = jax.vmap(vertical_slash)(subkeys)
    return patterns.reshape(PROMPT_COUNT, QUERY_HEADS, STRETCH_BLOCKS, PROMPT_BLOCKS).astype(jnp.int32)


def shuffle_pool(seed_key):
    return jax.random.permutation(seed_key, PREFIX_PAGES)


def draw_page_table(key, part):
    key = jax.random.fold_in(key, 31)
    subkeys = jax.random.split(key, REQUEST_GROUPS)
    orders = jax.vmap(shuffle_pool)(subkeys)
    return orders.reshape(PROMPT_COUNT, NBP).astype(jnp.int32)


def draw_prompt_lengths(key, part):
    key = jax.random.fold_in(key, 41)
    length_key, long_key, short_key = jax.random.split(key, 3)
    lengths = jax.random.randint(length_key, (PROMPT_COUNT,), 1, STRETCH_TOKENS + 1)
    longest = jax.random.randint(long_key, (), 0, PROMPT_COUNT)
    shortest = (longest + 1 + jax.random.randint(short_key, (), 0, PROMPT_COUNT - 1)) % PROMPT_COUNT
    request_ids = jnp.arange(PROMPT_COUNT)
    lengths = jnp.where(request_ids == longest, STRETCH_TOKENS, lengths)
    lengths = jnp.where(request_ids == shortest, 1, lengths)
    return lengths.astype(jnp.int32)


def placement_row(seed_key, target):
    order_key, slot_key = jax.random.split(seed_key)
    leading = jax.random.permutation(order_key, N_REQ)[:REQ_DEV]
    chosen_slot = jax.random.randint(slot_key, (), 0, REQ_DEV)
    present = jnp.any(leading == target)
    return jnp.where(present, leading, jnp.where(jnp.arange(REQ_DEV) == chosen_slot, target, leading))


def draw_placement(key, part):
    key = jax.random.fold_in(key, 51)
    target_key, row_key = jax.random.split(key)
    targets = jax.random.randint(target_key, (N_SECTION,), 0, N_REQ)
    row_targets = jnp.repeat(targets, N_REQ)
    subkeys = jax.random.split(row_key, REQUEST_GROUPS)
    return jax.vmap(placement_row)(subkeys, row_targets).astype(jnp.int32)


def quest_row(seed_key):
    return jax.random.permutation(seed_key, NBP)[:SELECTED_BLOCKS]


def draw_selected_prefix_blocks(key, part):
    key = jax.random.fold_in(key, 61)
    subkeys = jax.random.split(key, REQUEST_GROUPS * DECODE_SLOTS * DECODE_STEPS * QUERY_HEADS)
    selections = jax.vmap(quest_row)(subkeys)
    return selections.reshape(REQUEST_GROUPS, DECODE_SLOTS, DECODE_STEPS, QUERY_HEADS, SELECTED_BLOCKS).astype(jnp.int32)


def block_scale(rng, dims, cuts, low, largest):
    def one(axis_at, shards_of):
        heights = jax.random.uniform(jax.random.fold_in(jax.random.fold_in(rng, 6), axis_at), (shards_of,), jnp.float32, low / len(cuts), largest / len(cuts))
        return jnp.repeat(jnp.exp(heights), dims[axis_at] // shards_of).reshape((-1,) + (1,) * (len(dims) - axis_at - 1))

    factor_of = one(*cuts[0])
    for cut in cuts[1:]:
        factor_of = factor_of * one(*cut)
    return factor_of


def normal_values(stream_key, extent, scale, bound, cuts=(), held_as=jnp.bfloat16):
    values = scale * jax.random.normal(stream_key, extent, jnp.float32)
    if cuts:
        values = values * block_scale(stream_key, extent, cuts, -0.22, 0.18)
    return jnp.clip(values, -bound, bound).astype(held_as)


def setup_inputs(seed: int = 0) -> dict:
    key_of = jax.random.split(jax.random.key(seed), 11)
    return {
        "stretch_query": draw_stretch_query(jax.random.fold_in(key_of[10], 71), 0),
        "stretch_kv": draw_stretch_kv(jax.random.fold_in(key_of[10], 71), 0),
        "prefix_page_store": normal_values(key_of[2], (REQUEST_GROUPS * PREFIX_PAGES, BLOCK_TOKENS, KEY_VALUE_HEADS, 2 * HEAD_SIZE), 1.0, 6.0, ((0, 16), (2, 8))),
        "page_table": draw_page_table(jax.random.fold_in(key_of[10], 71), 0),
        "vs_mask": draw_vs_mask(jax.random.fold_in(key_of[10], 71), 0),
        "prompt_lengths": draw_prompt_lengths(jax.random.fold_in(key_of[10], 71), 0),
        "placement": draw_placement(jax.random.fold_in(key_of[10], 71), 0),
        "step_query_rows": draw_step_query_rows(jax.random.fold_in(key_of[10], 71), 0),
        "step_key_value": draw_step_key_value(jax.random.fold_in(key_of[10], 71), 0),
        "selected_prefix_blocks": draw_selected_prefix_blocks(jax.random.fold_in(key_of[10], 71), 0),
    }


rope_base = 500000.0

def rope_angles(positions):
    half_dim = HEAD_SIZE // 2
    frequency = jnp.exp(-math.log(rope_base) * (2.0 * jnp.arange(half_dim, dtype=jnp.float32) / HEAD_SIZE))
    angles = positions.astype(jnp.float32)[..., None] * frequency
    return (jnp.cos(angles), jnp.sin(angles))

def rotate_half(vectors, cos_part, sin_part):
    half_dim = vectors.shape[-1] // 2
    front_half = vectors[..., :half_dim]
    back_half = vectors[..., half_dim:]
    return jnp.concatenate([front_half * cos_part - back_half * sin_part, back_half * cos_part + front_half * sin_part], axis=-1)

def prefill_request(query_rows, stretch_query_rows, prefix_pages, block_mask):
    group_width = QUERY_HEADS // KEY_VALUE_HEADS
    positions = PRE + jnp.arange(STRETCH_TOKENS, dtype=jnp.int32)
    cos_part, sin_part = rope_angles(positions)
    query_matrix = query_rows.reshape(STRETCH_TOKENS, QUERY_HEADS, HEAD_SIZE).astype(jnp.float32)
    query_matrix = rotate_half(query_matrix, cos_part[:, None, :], sin_part[:, None, :]).astype(jnp.bfloat16)
    newest_keys = rotate_half(stretch_query_rows[..., :HEAD_SIZE].astype(jnp.float32), cos_part[:, None, :], sin_part[:, None, :]).astype(jnp.bfloat16)
    newest_pages = jnp.concatenate([newest_keys, stretch_query_rows[..., HEAD_SIZE:]], axis=-1).reshape(STRETCH_BLOCKS, BLOCK_TOKENS, KEY_VALUE_HEADS, 2 * HEAD_SIZE)
    prompt_page_list = jnp.concatenate([prefix_pages, newest_pages], axis=0)
    token_list = prompt_page_list.reshape(PROMPT_BLOCKS * BLOCK_TOKENS, KEY_VALUE_HEADS, 2 * HEAD_SIZE)
    grouped_heads = query_matrix.reshape(STRETCH_TOKENS, KEY_VALUE_HEADS, group_width, HEAD_SIZE).astype(jnp.float32)
    scores = jnp.einsum('ikgd,jkd->kgij', grouped_heads, token_list[..., :HEAD_SIZE].astype(jnp.float32)) / math.sqrt(HEAD_SIZE)
    key_positions = jnp.arange(PROMPT_BLOCKS * BLOCK_TOKENS, dtype=jnp.int32)
    causal_mask = key_positions[None, :] <= positions[:, None]
    allowed_mask = jnp.repeat(jnp.repeat(block_mask == 1, BLOCK_TOKENS, axis=1), BLOCK_TOKENS, axis=2)
    active_flag = (allowed_mask & causal_mask[None]).reshape(KEY_VALUE_HEADS, group_width, STRETCH_TOKENS, PROMPT_BLOCKS * BLOCK_TOKENS)
    row_peak = lax.optimization_barrier(jnp.max(jnp.where(active_flag, scores, -jnp.inf), axis=-1, keepdims=True))
    weights = jnp.where(active_flag, jnp.exp(scores - row_peak), 0.0)
    row_total = lax.optimization_barrier(jnp.sum(weights, axis=-1))
    rounded = lax.optimization_barrier(weights.astype(jnp.bfloat16)).astype(jnp.float32)
    attended = jnp.einsum('kgij,jkd->ikgd', rounded, token_list[..., HEAD_SIZE:].astype(jnp.float32))
    attended = attended / jnp.transpose(row_total, (2, 0, 1))[..., None]
    return (attended.reshape(STRETCH_TOKENS, QUERY_HEADS * HEAD_SIZE).astype(jnp.bfloat16), prompt_page_list)

def decode_slot(slot_page_list, overall_length, occupied_slots, query_matrix, new_rows, chosen):
    group_width = QUERY_HEADS // KEY_VALUE_HEADS
    positions = overall_length + jnp.arange(DECODE_STEPS, dtype=jnp.int32)
    cos_part, sin_part = rope_angles(positions)
    rotated_rows = rotate_half(query_matrix.reshape(DECODE_STEPS, QUERY_HEADS, HEAD_SIZE).astype(jnp.float32), cos_part[:, None, :], sin_part[:, None, :]).astype(jnp.bfloat16)
    new_keys = rotate_half(new_rows[..., :HEAD_SIZE].astype(jnp.float32), cos_part[:, None, :], sin_part[:, None, :]).astype(jnp.bfloat16)
    token_list = slot_page_list.reshape(PROMPT_BLOCKS * BLOCK_TOKENS, KEY_VALUE_HEADS, 2 * HEAD_SIZE)
    grouped_heads = rotated_rows.reshape(DECODE_STEPS, KEY_VALUE_HEADS, group_width, HEAD_SIZE).astype(jnp.float32)
    old_scores = jnp.einsum('ekgd,jkd->ekgj', grouped_heads, token_list[..., :HEAD_SIZE].astype(jnp.float32)) / math.sqrt(HEAD_SIZE)
    new_scores = jnp.einsum('ekgd,fkd->ekgf', grouped_heads, new_keys.astype(jnp.float32)) / math.sqrt(HEAD_SIZE)
    token_ids = jnp.arange(PROMPT_BLOCKS * BLOCK_TOKENS, dtype=jnp.int32)
    block_ids = token_ids // BLOCK_TOKENS
    picked = jnp.any(chosen[..., None] == block_ids, axis=-2)
    retained_mask = (token_ids < overall_length) & (picked & (block_ids < NBP) | (token_ids >= PRE))
    retained_mask = retained_mask.reshape(DECODE_STEPS, KEY_VALUE_HEADS, group_width, PROMPT_BLOCKS * BLOCK_TOKENS)
    step_ids = jnp.arange(DECODE_STEPS, dtype=jnp.int32)
    own_kept = jnp.broadcast_to((step_ids[None, :] <= step_ids[:, None])[:, None, None, :], new_scores.shape)
    all_scores = jnp.concatenate([old_scores, new_scores], axis=-1)
    all_kept = jnp.concatenate([retained_mask, own_kept], axis=-1)
    row_peak = lax.optimization_barrier(jnp.max(jnp.where(all_kept, all_scores, -jnp.inf), axis=-1, keepdims=True))
    weights = jnp.where(all_kept, jnp.exp(all_scores - row_peak), 0.0)
    row_total = lax.optimization_barrier(jnp.sum(weights, axis=-1))
    value_matrix = jnp.concatenate([token_list[..., HEAD_SIZE:], new_rows[..., HEAD_SIZE:]], axis=0).astype(jnp.float32)
    attended = jnp.einsum('ekgj,jkd->ekgd', weights, value_matrix, precision=lax.Precision.HIGHEST) / row_total[..., None]
    attended = jnp.where(occupied_slots, attended, 0.0)
    return attended.reshape(DECODE_STEPS, QUERY_HEADS * HEAD_SIZE).astype(jnp.bfloat16)

def reference(stretch_query, stretch_kv, prefix_page_store, page_table, vs_mask, prompt_lengths, placement, step_query_rows, step_key_value, selected_prefix_blocks):

    def prefill_one(request):
        prefill_group = request // REQ_DEV
        query_rows = lax.dynamic_slice_in_dim(stretch_query, request * STRETCH_TOKENS, STRETCH_TOKENS, 0)
        stretch_query_rows = lax.dynamic_slice_in_dim(stretch_kv, request * STRETCH_TOKENS, STRETCH_TOKENS, 0)
        table_row = lax.dynamic_index_in_dim(page_table, request, 0, keepdims=False)
        prefix_pages = jnp.take(prefix_page_store, prefill_group * PREFIX_PAGES + table_row, axis=0)
        block_mask = lax.dynamic_index_in_dim(vs_mask, request, 0, keepdims=False)
        return prefill_request(query_rows, stretch_query_rows, prefix_pages, block_mask)
    attended, prompt_page_list = lax.map(prefill_one, jnp.arange(PROMPT_COUNT, dtype=jnp.int32))
    prefill_out = attended.reshape(PROMPT_COUNT * STRETCH_TOKENS, QUERY_HEADS * HEAD_SIZE)
    decode_group = jnp.arange(REQUEST_GROUPS, dtype=jnp.int32)[:, None]
    slot_ids = jnp.arange(DECODE_SLOTS, dtype=jnp.int32)[None, :]
    source_rows = (1 - decode_group // N_REQ) * N_REQ + slot_ids
    matches = jnp.take(placement, source_rows, axis=0) == (decode_group % N_REQ)[..., None]
    occupied_slots = jnp.any(matches, axis=-1)
    chosen_index = jnp.argmax(matches.astype(jnp.int32), axis=-1).astype(jnp.int32)
    request_ids = source_rows * REQ_DEV + chosen_index
    slot_page_store = jnp.where(occupied_slots[..., None, None, None, None], jnp.take(prompt_page_list, request_ids, axis=0), jnp.zeros((), jnp.bfloat16))
    overall_length = PRE + jnp.take(prompt_lengths, request_ids)

    def decode_single(inputs):
        return decode_slot(*inputs)
    decode_output = lax.map(decode_single, (slot_page_store.reshape(REQUEST_GROUPS * DECODE_SLOTS, PROMPT_BLOCKS, BLOCK_TOKENS, KEY_VALUE_HEADS, 2 * HEAD_SIZE), overall_length.reshape(-1), occupied_slots.reshape(-1), step_query_rows.reshape(REQUEST_GROUPS * DECODE_SLOTS, DECODE_STEPS, QUERY_HEADS * HEAD_SIZE), step_key_value.reshape(REQUEST_GROUPS * DECODE_SLOTS, DECODE_STEPS, KEY_VALUE_HEADS, 2 * HEAD_SIZE), selected_prefix_blocks.reshape(REQUEST_GROUPS * DECODE_SLOTS, DECODE_STEPS, QUERY_HEADS, SELECTED_BLOCKS)))
    decode_output = decode_output.reshape(REQUEST_GROUPS, DECODE_SLOTS, DECODE_STEPS, QUERY_HEADS * HEAD_SIZE)
    return (prefill_out, slot_page_store, decode_output)
```

```python
import functools
import math

import jax
import jax.numpy as jnp
from jax import lax
from jax.experimental import pallas as pl
from jax.experimental.pallas import tpu as pltpu
from jax.sharding import PartitionSpec as P

QUERY_HEADS = 64
KEY_VALUE_HEADS = 8
HEAD_SIZE = 128
PRE = 1536
STRETCH_TOKENS = 512
BLOCK_TOKENS = 64
REQ_DEV = 4
DECODE_STEPS = 2
DECODE_SLOTS = 8
NBP = 24
STRETCH_BLOCKS = 8
PROMPT_BLOCKS = 32
SELECTED_BLOCKS = 8
PREFIX_PAGES = 96
HEADS = 8
PAGE = 2 * HEAD_SIZE
N_TP = 8
N_REQ = 8
RESULT_ROWS = 16
CHUNKS = (2, 2)
STARTS = tuple(sum(CHUNKS[:c]) for c in range(len(CHUNKS)))
HEADS_AT_ONCE = 4
ORDER = ('d@00', 'p0@04', 'r0', 'p1@10', 'p2@13', 'r1', 'p3', 's0', 's1')
QUERY_ROWS = 256

ROPE_BASE = 500000.0
OFF = -1e30
EXP2_SCALE = math.log2(math.e) / math.sqrt(HEAD_SIZE)
VMEM = 60 << 20
LIGHT = pl.CostEstimate(flops=1, bytes_accessed=1, transcendentals=0)

def all_places():
    for section in range(2):
        for req in range(N_REQ):
            for tp in range(N_TP):
                yield section, req, tp


def place_number(section, req, tp):
    return (section * N_REQ + req) * N_TP + tp


def other_side(req):
    return (req + N_REQ // 2) % N_REQ


TP_OFFSETS = [(dz, dc) for dz in range(4) for dc in range(2)]


def tp_moved(tp, offset, sign=1):
    dz, dc = offset
    return (tp // 2 + sign * dz + 4) % 4 * 2 + (tp + dc) % 2


def cross_route(offset):
    return [
        (place_number(s, r, t), place_number(1 - s, other_side(r), tp_moved(t, offset)))
        for s, r, t in all_places()
    ]


def routed_rows(c):
    extra = DECODE_STEPS * HEADS // 2 if c == len(CHUNKS) - 1 else 0
    return (CHUNKS[c] * BLOCK_TOKENS + extra) * HEADS


def travelling_rows(c):
    return CHUNKS[c] * BLOCK_TOKENS + (RESULT_ROWS if c == len(CHUNKS) - 1 else 0)


def rope_tables(positions):
    half = HEAD_SIZE // 2
    frequency = jnp.exp(
        -math.log(ROPE_BASE) * (2.0 * jnp.arange(half, dtype=jnp.float32) / HEAD_SIZE)
    )
    angles = positions.astype(jnp.float32)[..., None] * frequency
    cos_part, sin_part = jnp.cos(angles), jnp.sin(angles)
    return (
        jnp.concatenate([cos_part, cos_part], -1),
        jnp.concatenate([-sin_part, sin_part], -1),
    )


def rotated(rows, cos_part, sin_part):
    rows = rows.astype(jnp.float32)
    return (rows * cos_part + pltpu.roll(rows, HEAD_SIZE // 2, 1) * sin_part).astype(jnp.bfloat16)


def assemble_kernel(target_ref, table_ref, prefix_ref, kv_ref, cos_ref, sin_ref, *refs):
    chunks = range(len(CHUNKS))
    own, outs, (held, arrive, leave) = refs[0], refs[1:-3], refs[-3:]
    copies = [[] for _ in chunks]
    for c, count in enumerate(CHUNKS):
        for target in range(NBP // 4):
            for prompt in range(REQ_DEV):
                for b in range(count):
                    block = target * 4 + STARTS[c] + b
                    place = held.at[prompt, pl.ds(block * BLOCK_TOKENS, BLOCK_TOKENS)]
                    page = table_ref[prompt * NBP + block]
                    copies[c].append(
                        pltpu.make_async_copy(prefix_ref.at[page], place, arrive.at[c])
                    )
                    copies[c][-1].start()
    for prompt in range(REQ_DEV):
        rows = slice(prompt * STRETCH_TOKENS, (prompt + 1) * STRETCH_TOKENS)
        held[prompt, PRE:, :HEAD_SIZE] = rotated(
            kv_ref[rows, :HEAD_SIZE], cos_ref[...], sin_ref[...]
        )
        held[prompt, PRE:, HEAD_SIZE:] = kv_ref[rows, HEAD_SIZE:]
    out_copies = []
    for c, count in enumerate(CHUNKS):
        size = count * BLOCK_TOKENS
        for copy in copies[c]:
            copy.wait()
        for j in range(N_TP):
            first = (target_ref[j] * 4 + STARTS[c]) * BLOCK_TOKENS
            out_copies.append(
                pltpu.make_async_copy(
                    held.at[:, pl.ds(pl.multiple_of(first, BLOCK_TOKENS), size)],
                    outs[c * N_TP + j].at[:, pl.ds(0, size)],
                    leave.at[c],
                )
            )
            out_copies[-1].start()
    out_copies.append(pltpu.make_async_copy(held, own, leave.at[len(CHUNKS)]))
    out_copies[-1].start()
    for copy in out_copies:
        copy.wait()


def assembled(targets, table, prefix, kv, cos_part, sin_part):
    anywhere = pl.BlockSpec(memory_space=pltpu.HBM)
    whole = pl.BlockSpec(memory_space=pltpu.VMEM)
    scalars = pl.BlockSpec(memory_space=pltpu.SMEM)
    own = (REQ_DEV, PROMPT_BLOCKS * BLOCK_TOKENS, PAGE)
    shapes = [own] + [
        (REQ_DEV, travelling_rows(c), PAGE) for c in range(len(CHUNKS)) for _ in range(N_TP)
    ]
    outs = pl.pallas_call(
        assemble_kernel,
        in_specs=[scalars, scalars, anywhere, whole, whole, whole],
        out_specs=[anywhere] * len(shapes),
        out_shape=[jax.ShapeDtypeStruct(shape, jnp.bfloat16) for shape in shapes],
        scratch_shapes=[
            pltpu.VMEM(own, jnp.bfloat16),
            pltpu.SemaphoreType.DMA((len(CHUNKS),)),
            pltpu.SemaphoreType.DMA((len(CHUNKS) + 1,)),
        ],
        compiler_params=pltpu.CompilerParams(vmem_limit_bytes=VMEM),
        cost_estimate=LIGHT,
        name="assembled",
    )(targets, table, prefix, kv, cos_part, sin_part)
    return outs[0], [outs[1 + c * N_TP : 1 + (c + 1) * N_TP] for c in range(len(CHUNKS))]


def route_kernel(width, group_ref, prompt_ref, head_ref, *refs):
    arrived, (out, spread, packed, empty, sem) = refs[:N_TP], refs[N_TP:]
    prompt = pl.program_id(0)
    rows = width // HEADS

    @pl.when(prompt == 0)
    def _():
        empty[...] = jnp.zeros_like(empty)
        for d in range(N_REQ):

            @pl.when(prompt_ref[d] < 0)
            def _():
                pltpu.make_async_copy(empty, out.at[d], sem).start()

    for first in range(0, rows, BLOCK_TOKENS):
        size = min(BLOCK_TOKENS, rows - first)
        for half in range(2):
            lanes = pl.ds(half * HEAD_SIZE, HEAD_SIZE)
            for j in range(N_TP):
                places = pl.ds(first * HEADS + head_ref[j], size, stride=HEADS)
                block = arrived[j][0, pl.ds(first, max(size, RESULT_ROWS)), lanes]
                spread[half, places, :] = block.astype(jnp.float32)[:size]
            part = pl.ds(first * HEADS, size * HEADS)
            packed[prompt, part, lanes] = spread[half, part, :].astype(jnp.bfloat16)
    pltpu.make_async_copy(packed.at[prompt], out.at[group_ref[prompt]], sem).start()

    @pl.when(prompt == REQ_DEV - 1)
    def _():
        pltpu.make_async_copy(out, out, sem).wait()


def routed_pages(c, targets, prompts, heads, arrived):
    rows, width = travelling_rows(c), routed_rows(c)
    return pl.pallas_call(
        functools.partial(route_kernel, width),
        grid_spec=pltpu.PrefetchScalarGridSpec(
            num_scalar_prefetch=3,
            grid=(REQ_DEV,),
            in_specs=[pl.BlockSpec((1, rows, PAGE), lambda n, *_: (n, 0, 0))] * N_TP,
            out_specs=pl.BlockSpec(memory_space=pltpu.HBM),
            scratch_shapes=[
                pltpu.VMEM((2, width, HEAD_SIZE), jnp.float32),
                pltpu.VMEM((REQ_DEV, width, PAGE), jnp.bfloat16),
                pltpu.VMEM((width, PAGE), jnp.bfloat16),
                pltpu.SemaphoreType.DMA,
            ],
        ),
        out_shape=jax.ShapeDtypeStruct((N_REQ, width, PAGE), jnp.bfloat16),
        compiler_params=pltpu.CompilerParams(vmem_limit_bytes=VMEM),
        cost_estimate=LIGHT,
        name="routed_pages",
    )(targets, prompts, heads, *arrived)


def store_kernel(c, pieces, *refs):
    out, held, arrive, leave = refs[-4:]
    rows = CHUNKS[c] * BLOCK_TOKENS * HEADS
    place = pl.ds(STARTS[c] * BLOCK_TOKENS * HEADS, rows)
    ins, outs = [], []
    for slot in range(DECODE_SLOTS):
        source = pieces.at[other_side(slot), pl.ds(0, rows)]
        ins.append(pltpu.make_async_copy(source, held.at[slot], arrive.at[slot]))
        outs.append(pltpu.make_async_copy(held.at[slot], out.at[slot, place], leave.at[slot]))
    for copy in ins:
        copy.start()
    for slot in range(DECODE_SLOTS):
        ins[slot].wait()
        outs[slot].start()
    for copy in outs:
        copy.wait()


def stored_chunk(c, pieces, store):
    rows = CHUNKS[c] * BLOCK_TOKENS * HEADS
    operands = [pieces] + ([] if store is None else [store])
    anywhere = pl.BlockSpec(memory_space=pltpu.HBM)
    return pl.pallas_call(
        functools.partial(store_kernel, c),
        in_specs=[anywhere] * len(operands),
        out_specs=anywhere,
        out_shape=jax.ShapeDtypeStruct(
            (DECODE_SLOTS, 4 * BLOCK_TOKENS * HEADS, PAGE), jnp.bfloat16
        ),
        scratch_shapes=[
            pltpu.VMEM((DECODE_SLOTS, rows, PAGE), jnp.bfloat16),
            pltpu.SemaphoreType.DMA((DECODE_SLOTS,)),
            pltpu.SemaphoreType.DMA((DECODE_SLOTS,)),
        ],
        input_output_aliases={} if store is None else {1: 0},
        compiler_params=pltpu.CompilerParams(vmem_limit_bytes=VMEM),
        cost_estimate=LIGHT,
        name="stored_chunk",
    )(*operands)


def prefill_kernel(mask_ref, query_ref, cos_ref, sin_ref, *refs):
    page_ref = refs[0]
    out_ref, keys, values = refs[-3:]
    tokens = PROMPT_BLOCKS * BLOCK_TOKENS

    @pl.when(pl.program_id(0) == 0)
    def _():
        keys[:, :HEAD_SIZE] = page_ref[0, :, :HEAD_SIZE]
        values[:, :HEAD_SIZE] = page_ref[0, :, HEAD_SIZE:]
        block = lax.broadcasted_iota(jnp.int32, (tokens, HEAD_SIZE), 0) // BLOCK_TOKENS
        lane = lax.broadcasted_iota(jnp.int32, (tokens, HEAD_SIZE), 1)
        keys[:, HEAD_SIZE:] = jnp.where(block == lane, 1.0, 0.0).astype(jnp.bfloat16)
        values[:, HEAD_SIZE:] = jnp.ones((tokens, HEAD_SIZE), jnp.bfloat16)

    row = lax.broadcasted_iota(jnp.int32, (BLOCK_TOKENS, HEAD_SIZE), 0)
    column = lax.broadcasted_iota(jnp.int32, (BLOCK_TOKENS, HEAD_SIZE), 1)

    def masked_scores(head, first):
        lanes = slice(head * HEAD_SIZE, (head + 1) * HEAD_SIZE)
        rows = slice(first, first + QUERY_ROWS)
        blocks = range(first // BLOCK_TOKENS, (first + QUERY_ROWS) // BLOCK_TOKENS)
        width = PRE + -(-(first + QUERY_ROWS) // HEAD_SIZE) * HEAD_SIZE
        query = rotated(query_ref[rows, lanes], cos_ref[rows, :], sin_ref[rows, :])
        mask = jnp.concatenate(
            [
                jnp.broadcast_to(mask_ref[head, a : a + 1, :], (BLOCK_TOKENS, HEAD_SIZE))
                for a in blocks
            ],
            0,
        ).astype(jnp.bfloat16)
        scores = lax.dot_general(
            jnp.concatenate([query, mask], 1),
            keys[:width, :],
            (((1,), (1,)), ((), ())),
            preferred_element_type=jnp.float32,
        )
        parts = []
        for i, a in enumerate(blocks):
            part = scores[i * BLOCK_TOKENS : (i + 1) * BLOCK_TOKENS]
            start = PRE + a * BLOCK_TOKENS
            left = start // HEAD_SIZE * HEAD_SIZE
            right = left + HEAD_SIZE
            causal = column - (start - left) <= row
            pieces = [part[:, :left], jnp.where(causal, part[:, left:right], OFF)]
            if right < width:
                pieces.append(part[:, right:])
            parts.append(jnp.concatenate(pieces, 1))
        return jnp.concatenate(parts, 0)

    def attend(head, first, scores):
        peak = jnp.max(scores, axis=1, keepdims=True)
        weights = jnp.exp2((scores - peak) * EXP2_SCALE).astype(jnp.bfloat16)
        result = lax.dot_general(
            weights,
            values[: scores.shape[1], :],
            (((1,), (0,)), ((), ())),
            preferred_element_type=jnp.float32,
        )
        out_ref[first : first + QUERY_ROWS, head * HEAD_SIZE : (head + 1) * HEAD_SIZE] = (
            result[:, :HEAD_SIZE] / result[:, HEAD_SIZE:]
        ).astype(jnp.bfloat16)

    before = None
    for head in range(HEADS_AT_ONCE):
        for first in range(0, STRETCH_TOKENS, QUERY_ROWS):
            current = (head, first, masked_scores(head, first))
            if before is not None:
                attend(*before)
            before = current
    attend(*before)


def prefill_prompt(prompt, mask, query, cos_part, sin_part, pages, out):
    tables = pl.BlockSpec((STRETCH_TOKENS, HEAD_SIZE), lambda i: (0, 0))
    rows = pl.BlockSpec((STRETCH_TOKENS, HEADS_AT_ONCE * HEAD_SIZE), lambda i: (prompt, i))
    steps = HEADS // HEADS_AT_ONCE
    operands = [mask, query, cos_part, sin_part, pages] + ([] if out is None else [out])
    return pl.pallas_call(
        prefill_kernel,
        grid=(steps,),
        in_specs=[
            pl.BlockSpec(
                (HEADS_AT_ONCE, STRETCH_BLOCKS, HEAD_SIZE), lambda i: (prompt * steps + i, 0, 0)
            ),
            rows,
            tables,
            tables,
        ]
        + [pl.BlockSpec((1, PROMPT_BLOCKS * BLOCK_TOKENS, PAGE), lambda i: (prompt, 0, 0))]
        + ([] if out is None else [pl.BlockSpec(memory_space=pltpu.HBM)]),
        out_specs=rows,
        out_shape=jax.ShapeDtypeStruct(query.shape, query.dtype),
        scratch_shapes=[pltpu.VMEM((PROMPT_BLOCKS * BLOCK_TOKENS, PAGE), jnp.bfloat16)] * 2,
        input_output_aliases={} if out is None else {len(operands) - 1: 0},
        compiler_params=pltpu.CompilerParams(vmem_limit_bytes=VMEM),
        cost_estimate=LIGHT,
        name="prefill_prompt",
    )(*operands)


def decode_kernel(length_ref, query_ref, fresh_ref, cos_ref, sin_ref, picked_ref, *refs):
    page_ref, outs = refs[0], refs[-N_TP:]
    prompt = pl.program_id(0)
    lines = DECODE_STEPS * HEADS
    tokens = PROMPT_BLOCKS * BLOCK_TOKENS
    width = tokens + HEAD_SIZE

    def by_step(array, rows, step):
        return jnp.where(step == 0, array[0:1], array[1:2])

    line = lax.broadcasted_iota(jnp.int32, (lines, HEAD_SIZE), 0)
    line_step = line % HEADS // (HEADS // 2)
    query = rotated(
        query_ref[0],
        by_step(cos_ref[0], lines, line_step),
        by_step(sin_ref[0], lines, line_step),
    )
    place = lax.broadcasted_iota(jnp.int32, (HEAD_SIZE, HEAD_SIZE), 0)
    fresh = fresh_ref[0].astype(jnp.float32)
    cos_part, sin_part = (by_step(r[0], HEAD_SIZE, place) for r in (cos_ref, sin_ref))
    fresh_keys = by_step(fresh[:, :HEAD_SIZE], HEAD_SIZE, place)
    fresh_keys = rotated(jnp.where(place < DECODE_STEPS, fresh_keys, 0.0), cos_part, sin_part)
    fresh_values = by_step(fresh[:, HEAD_SIZE:], HEAD_SIZE, place)
    fresh_values = jnp.where(place < DECODE_STEPS, fresh_values, 0.0).astype(jnp.bfloat16)
    keys = jnp.concatenate([page_ref[0, :, :HEAD_SIZE], fresh_keys], 0)
    values = jnp.concatenate([page_ref[0, :, HEAD_SIZE:], fresh_values], 0)
    scores = lax.dot_general(
        query, keys, (((1,), (1,)), ((), ())), preferred_element_type=jnp.float32
    )
    number = lax.broadcasted_iota(jnp.int32, (lines, width), 1)
    block = number // BLOCK_TOKENS
    step = lax.broadcasted_iota(jnp.int32, (lines, width), 0) % HEADS // (HEADS // 2)
    picked = picked_ref[0]
    kept = block >= NBP
    for i in range(SELECTED_BLOCKS):
        kept = kept | (picked[:, i : i + 1] == block)
    kept = kept & (number < length_ref[prompt])
    kept = (kept & (number < tokens)) | ((number >= tokens) & (number - tokens <= step))
    scores = jnp.where(kept, scores, OFF)
    peak = jnp.max(scores, axis=1, keepdims=True)
    weights = jnp.where(kept, jnp.exp2((scores - peak) * EXP2_SCALE), 0.0)
    total = jnp.sum(weights, axis=1, keepdims=True)
    coarse = weights.astype(jnp.bfloat16)
    fine = (weights - coarse.astype(jnp.float32)).astype(jnp.bfloat16)
    result = lax.dot_general(
        jnp.concatenate([coarse, fine], 0),
        values,
        (((1,), (0,)), ((), ())),
        preferred_element_type=jnp.float32,
    )
    result = (result[:lines] + result[lines:]) / total
    result = jnp.concatenate([result[:HEADS], result[HEADS:]], 1)
    result = jnp.concatenate([result, jnp.zeros_like(result)], 0).astype(jnp.bfloat16)
    for out in outs:
        out[0] = result


def decoded(lengths, query, fresh, cos_part, sin_part, picked, pages, leaving):
    def one(array):
        return pl.BlockSpec((1,) + array.shape[1:], lambda n, *_: (n, 0, 0))

    operands = [query, fresh, cos_part, sin_part, picked, pages]
    place = CHUNKS[-1] * BLOCK_TOKENS // RESULT_ROWS
    return pl.pallas_call(
        decode_kernel,
        grid_spec=pltpu.PrefetchScalarGridSpec(
            num_scalar_prefetch=1,
            grid=(REQ_DEV,),
            in_specs=[one(x) for x in operands] + [pl.BlockSpec(memory_space=pltpu.HBM)] * N_TP,
            out_specs=[pl.BlockSpec((1, RESULT_ROWS, PAGE), lambda n, *_: (n, place, 0))] * N_TP,
        ),
        out_shape=[jax.ShapeDtypeStruct(x.shape, jnp.bfloat16) for x in leaving],
        input_output_aliases={1 + len(operands) + j: j for j in range(N_TP)},
        compiler_params=pltpu.CompilerParams(vmem_limit_bytes=VMEM),
        cost_estimate=LIGHT,
        name="decoded",
    )(lengths, *operands, *leaving)


def after(array, *others):
    return lax.optimization_barrier((array, *others))[0]


def shards(
    stretch_query,
    stretch_kv,
    prefix_page_store,
    page_table,
    vs_mask,
    prompt_lengths,
    placement,
    step_query_rows,
    step_key_value,
    selected_prefix_blocks,
):
    axes = ("section", "req", "tp")
    section = lax.axis_index("section")
    req = lax.axis_index("req")
    tp = lax.axis_index("tp")
    last = len(CHUNKS) - 1

    def across(leaving):
        return [
            lax.ppermute(pages, axes, cross_route(offset))
            for pages, offset in zip(leaving, TP_OFFSETS)
        ]

    cos_part, sin_part = rope_tables(PRE + jnp.arange(STRETCH_TOKENS, dtype=jnp.int32))
    tp_targets = jnp.stack([tp_moved(tp, offset) for offset in TP_OFFSETS]).astype(jnp.int32)
    pages, leaving = assembled(
        tp_targets,
        page_table.reshape(-1),
        prefix_page_store.reshape(PREFIX_PAGES, BLOCK_TOKENS, PAGE),
        stretch_kv.reshape(-1, PAGE),
        cos_part,
        sin_part,
    )
    arrived = [across(chunk) for chunk in leaving[:last]]

    own_heads = HEADS * HEAD_SIZE
    queries = lax.dynamic_slice_in_dim(after(step_query_rows, pages)[0], tp * own_heads, own_heads, 2)
    fresh = lax.dynamic_index_in_dim(step_key_value[0], tp, 2, keepdims=False)
    picks = lax.dynamic_slice_in_dim(selected_prefix_blocks[0], tp * HEADS, HEADS, 2)
    load = jnp.concatenate(
        [queries, fresh, picks.astype(jnp.bfloat16).reshape(DECODE_SLOTS, DECODE_STEPS, -1)],
        axis=-1,
    )
    sections = jnp.arange(2, dtype=jnp.int32)[:, None, None, None]
    load = jnp.where(sections == 1 - section, load[None], jnp.zeros((), load.dtype))
    load = lax.all_to_all(
        load.reshape((2 * N_REQ,) + load.shape[2:]),
        ("section", "req"),
        split_axis=0,
        concat_axis=0,
        tiled=True,
    )

    mask = jnp.where(vs_mask == 1, 0.0, OFF).reshape(-1, STRETCH_BLOCKS, PROMPT_BLOCKS)
    mask = jnp.pad(mask, ((0, 0), (0, 0), (0, HEAD_SIZE - PROMPT_BLOCKS)))

    def prefilled(prompt, out, *others):
        return prefill_prompt(
            prompt, after(mask, *others), stretch_query, cos_part, sin_part, pages, out
        )

    own_row = section * N_REQ + req
    targets = lax.dynamic_index_in_dim(placement, own_row, 0, keepdims=False)
    load = jnp.take(load, (1 - section) * N_REQ + targets, axis=0)
    lengths = PRE + lax.dynamic_slice_in_dim(prompt_lengths, own_row * REQ_DEV, REQ_DEV, 0)
    steps = jnp.arange(DECODE_STEPS, dtype=jnp.int32)
    step_cos, step_sin = rope_tables(lengths[:, None] + steps)

    def by_line(array):
        array = array.reshape(REQ_DEV, DECODE_STEPS, HEADS // 2, 2, -1)
        return jnp.transpose(array, (0, 3, 1, 2, 4)).reshape(REQ_DEV, DECODE_STEPS * HEADS, -1)

    origin = (1 - section) * N_REQ + other_side(req)
    origin_targets = lax.dynamic_index_in_dim(placement, origin, 0, keepdims=False)
    number = jnp.arange(REQ_DEV, dtype=jnp.int32)
    group = jnp.arange(N_REQ, dtype=jnp.int32)
    prompts = jnp.max(jnp.where(origin_targets == group[:, None], number, -1), axis=-1)

    def over_req(pages):
        return lax.all_to_all(pages, "req", split_axis=0, concat_axis=0, tiled=True)

    heads = jnp.stack([tp_moved(tp, offset, -1) for offset in TP_OFFSETS]).astype(jnp.int32)
    prefill_out = None
    waiting = []
    store = None
    before = None
    for step in ORDER:
        step, _, piece = step.partition("@")
        kind, n = step[0], int(step[1:] or 0)
        others = () if before is None else (before,)
        if piece:
            others += (arrived[int(piece[0])][int(piece[1])],)
        if kind == "d":
            full_last = decoded(
                after(lengths, *others),
                by_line(load[..., :own_heads]),
                load[..., own_heads : own_heads + PAGE],
                step_cos,
                step_sin,
                by_line(load[..., own_heads + PAGE :]).astype(jnp.int32),
                pages,
                leaving[last],
            )
            arrived.append(across(full_last))
            before = full_last[0]
        elif kind == "r":
            chunk = list(arrived[n])
            chunk[0] = after(chunk[0], *others)
            before = routed_pages(n, origin_targets, prompts, heads, chunk)
            waiting.append(over_req(before))
        elif kind == "p":
            before = prefill_out = prefilled(n, prefill_out, *others)
        else:
            before = store = stored_chunk(n, after(waiting[n], *others), store)
    routed = waiting[last]
    store = store.reshape(1, DECODE_SLOTS, 4, BLOCK_TOKENS, KEY_VALUE_HEADS, PAGE)
    first = CHUNKS[last] * BLOCK_TOKENS * HEADS
    results = routed[:, first : first + HEADS * KEY_VALUE_HEADS]
    results = results.reshape(2, N_REQ // 2, DECODE_STEPS, HEADS // 2, KEY_VALUE_HEADS, PAGE)
    results = jnp.transpose(results[::-1], (0, 1, 2, 4, 3, 5))
    decode_output = results.reshape(1, DECODE_SLOTS, DECODE_STEPS, QUERY_HEADS * HEAD_SIZE)
    return (prefill_out, store, decode_output)


def solution(mesh):
    placed = (
        P(("section", "req"), "tp"),
        P(("section", "req"), "tp", None),
        P(("section", "req"), None, "tp", None),
        P(("section", "req"), None),
        P(("section", "req"), "tp", None, None),
        P(),
        P(),
        P(("section", "req"), None, None, None),
        P(("section", "req"), None, None, None, None),
        P(("section", "req"), None, None, None, None),
    )
    return jax.shard_map(
        shards,
        mesh=mesh,
        in_specs=placed,
        out_specs=(
            P(("section", "req"), "tp"),
            P(("section", "req"), None, "tp", None, None, None),
            P(("section", "req"), None, None, None),
        ),
        check_vma=False,
    )
```

```python
import functools
import math

import jax
import jax.numpy as jnp
from jax import lax
from jax.experimental import pallas as pl
from jax.experimental.pallas import tpu as pltpu
from jax.sharding import PartitionSpec as P

QUERY_HEADS = 64
KEY_VALUE_HEADS = 8
HEAD_SIZE = 128
PRE = 1536
STRETCH_TOKENS = 512
BLOCK_TOKENS = 64
REQ_DEV = 4
DECODE_STEPS = 2
DECODE_SLOTS = 8
NBP = 24
STRETCH_BLOCKS = 8
PROMPT_BLOCKS = 32
SELECTED_BLOCKS = 8
PREFIX_PAGES = 96
HEADS = 8
PAGE = 2 * HEAD_SIZE
N_TP = 8
N_REQ = 8
RESULT_ROWS = 16
CHUNKS = (2, 1, 1)
LAST = 1
AHEAD = 2
STARTS = tuple(sum(CHUNKS[:c]) for c in range(len(CHUNKS)))
HEADS_AT_ONCE = 4
ORDER = ('a@01', 'd', 'p0@05', 'r0@a', 'p1@10', 'P1', 'p4', 'r1@0', 'p5', 's0', 'p6', 's2@x', 'p7', 's1')
QUERY_ROWS = 256
PARTS = HEADS // HEADS_AT_ONCE

ROPE_BASE = 500000.0
OFF = -1e30
EXP2_SCALE = math.log2(math.e) / math.sqrt(HEAD_SIZE)
VMEM = 60 << 20
LIGHT = pl.CostEstimate(flops=1, bytes_accessed=1, transcendentals=0)

def all_places():
    for section in range(2):
        for req in range(N_REQ):
            for tp in range(N_TP):
                yield section, req, tp


def place_number(section, req, tp):
    return (section * N_REQ + req) * N_TP + tp


def other_side(req):
    return (req + N_REQ // 2) % N_REQ


TP_OFFSETS = [(dz, dc) for dz in range(4) for dc in range(2)]


def tp_moved(tp, offset, sign=1):
    dz, dc = offset
    return (tp // 2 + sign * dz + 4) % 4 * 2 + (tp + dc) % 2


def cross_route(offset):
    return [
        (place_number(s, r, t), place_number(1 - s, other_side(r), tp_moved(t, offset)))
        for s, r, t in all_places()
    ]


def routed_rows(c):
    extra = DECODE_STEPS * HEADS // 2 if c == LAST else 0
    return (CHUNKS[c] * BLOCK_TOKENS + extra) * HEADS


def travelling_rows(c):
    return CHUNKS[c] * BLOCK_TOKENS + (RESULT_ROWS if c == LAST else 0)


def rope_tables(positions):
    half = HEAD_SIZE // 2
    frequency = jnp.exp(
        -math.log(ROPE_BASE) * (2.0 * jnp.arange(half, dtype=jnp.float32) / HEAD_SIZE)
    )
    angles = positions.astype(jnp.float32)[..., None] * frequency
    cos_part, sin_part = jnp.cos(angles), jnp.sin(angles)
    return (
        jnp.concatenate([cos_part, cos_part], -1),
        jnp.concatenate([-sin_part, sin_part], -1),
    )


def rotated(rows, cos_part, sin_part):
    rows = rows.astype(jnp.float32)
    return (rows * cos_part + pltpu.roll(rows, HEAD_SIZE // 2, 1) * sin_part).astype(jnp.bfloat16)


def assemble_kernel(target_ref, table_ref, prefix_ref, kv_ref, cos_ref, sin_ref, *refs):
    chunks = range(len(CHUNKS))
    own, outs, (held, arrive, leave) = refs[0], refs[1:-3], refs[-3:]
    copies = [[] for _ in chunks]
    for c, count in enumerate(CHUNKS):
        for target in range(NBP // 4):
            for prompt in range(REQ_DEV):
                for b in range(count):
                    block = target * 4 + STARTS[c] + b
                    place = held.at[prompt, pl.ds(block * BLOCK_TOKENS, BLOCK_TOKENS)]
                    page = table_ref[prompt, block]
                    copies[c].append(
                        pltpu.make_async_copy(prefix_ref.at[page], place, arrive.at[c])
                    )
                    copies[c][-1].start()
    for prompt in range(REQ_DEV):
        rows = slice(prompt * STRETCH_TOKENS, (prompt + 1) * STRETCH_TOKENS)
        held[prompt, PRE:, :HEAD_SIZE] = rotated(
            kv_ref[rows, :HEAD_SIZE], cos_ref[...], sin_ref[...]
        )
        held[prompt, PRE:, HEAD_SIZE:] = kv_ref[rows, HEAD_SIZE:]
    out_copies = []
    for c, count in enumerate(CHUNKS):
        size = count * BLOCK_TOKENS
        for copy in copies[c]:
            copy.wait()
        for j in range(N_TP):
            target = j if c == AHEAD else target_ref[j]
            first = (target * 4 + STARTS[c]) * BLOCK_TOKENS
            if c != AHEAD:
                first = pl.multiple_of(first, BLOCK_TOKENS)
            out_copies.append(
                pltpu.make_async_copy(
                    held.at[:, pl.ds(first, size)],
                    outs[-1].at[j] if c == AHEAD else outs[c * N_TP + j].at[:, pl.ds(0, size)],
                    leave.at[c],
                )
            )
            out_copies[-1].start()
    out_copies.append(pltpu.make_async_copy(held, own, leave.at[len(CHUNKS)]))
    out_copies[-1].start()
    for copy in out_copies:
        copy.wait()


def assembled(targets, table, prefix, kv, cos_part, sin_part):
    anywhere = pl.BlockSpec(memory_space=pltpu.HBM)
    whole = pl.BlockSpec(memory_space=pltpu.VMEM)
    scalars = pl.BlockSpec(memory_space=pltpu.SMEM)
    own = (REQ_DEV, PROMPT_BLOCKS * BLOCK_TOKENS, PAGE)
    shapes = [own] + [
        (REQ_DEV, travelling_rows(c), PAGE) for c in range(AHEAD) for _ in range(N_TP)
    ]
    shapes.append((N_TP, REQ_DEV, travelling_rows(AHEAD), PAGE))
    outs = pl.pallas_call(
        assemble_kernel,
        in_specs=[scalars, scalars, anywhere, whole, whole, whole],
        out_specs=[anywhere] * len(shapes),
        out_shape=[jax.ShapeDtypeStruct(shape, jnp.bfloat16) for shape in shapes],
        scratch_shapes=[
            pltpu.VMEM(own, jnp.bfloat16),
            pltpu.SemaphoreType.DMA((len(CHUNKS),)),
            pltpu.SemaphoreType.DMA((len(CHUNKS) + 1,)),
        ],
        compiler_params=pltpu.CompilerParams(vmem_limit_bytes=VMEM),
        cost_estimate=LIGHT,
        name="assembled",
    )(targets, table, prefix, kv, cos_part, sin_part)
    chunks = [outs[1 + c * N_TP : 1 + (c + 1) * N_TP] for c in range(AHEAD)]
    return outs[0], chunks, outs[-1]


def route_kernel(width, group_ref, prompt_ref, head_ref, *refs):
    arrived, (out, spread, packed, empty, sem) = refs[:-5], refs[-5:]
    prompt = pl.program_id(0)
    rows = width // HEADS

    @pl.when(prompt == 0)
    def _():
        empty[...] = jnp.zeros_like(empty)
        for d in range(N_REQ):

            @pl.when(prompt_ref[d] < 0)
            def _():
                pltpu.make_async_copy(empty, out.at[d], sem).start()

    for first in range(0, rows, BLOCK_TOKENS):
        size = min(BLOCK_TOKENS, rows - first)
        for half in range(2):
            lanes = pl.ds(half * HEAD_SIZE, HEAD_SIZE)
            for j in range(N_TP):
                part = pl.ds(first, max(size, RESULT_ROWS))
                if len(arrived) == 1:
                    block = arrived[0][j, 0, part, lanes]
                else:
                    block = arrived[j][0, part, lanes]
                places = pl.ds(first * HEADS + head_ref[j], size, stride=HEADS)
                spread[half, places, :] = block.astype(jnp.float32)[:size]
            part = pl.ds(first * HEADS, size * HEADS)
            packed[prompt, part, lanes] = spread[half, part, :].astype(jnp.bfloat16)
    pltpu.make_async_copy(packed.at[prompt], out.at[group_ref[prompt]], sem).start()

    @pl.when(prompt == REQ_DEV - 1)
    def _():
        pltpu.make_async_copy(out, out, sem).wait()


def routed_pages(c, targets, prompts, heads, arrived):
    rows, width = travelling_rows(c), routed_rows(c)
    return pl.pallas_call(
        functools.partial(route_kernel, width),
        grid_spec=pltpu.PrefetchScalarGridSpec(
            num_scalar_prefetch=3,
            grid=(REQ_DEV,),
            in_specs=[pl.BlockSpec((N_TP, 1, rows, PAGE), lambda n, *_: (0, n, 0, 0))]
            if c == AHEAD
            else [pl.BlockSpec((1, rows, PAGE), lambda n, *_: (n, 0, 0))] * N_TP,
            out_specs=pl.BlockSpec(memory_space=pltpu.HBM),
            scratch_shapes=[
                pltpu.VMEM((2, width, HEAD_SIZE), jnp.float32),
                pltpu.VMEM((REQ_DEV, width, PAGE), jnp.bfloat16),
                pltpu.VMEM((width, PAGE), jnp.bfloat16),
                pltpu.SemaphoreType.DMA,
            ],
        ),
        out_shape=jax.ShapeDtypeStruct((N_REQ, width, PAGE), jnp.bfloat16),
        compiler_params=pltpu.CompilerParams(vmem_limit_bytes=VMEM),
        cost_estimate=LIGHT,
        name="routed_pages",
    )(targets, prompts, heads, *arrived)


def store_kernel(c, pieces, *refs):
    out, held, arrive, leave = refs[-4:]
    rows = CHUNKS[c] * BLOCK_TOKENS * HEADS
    place = pl.ds(STARTS[c] * BLOCK_TOKENS * HEADS, rows)
    ins, outs = [], []
    for slot in range(DECODE_SLOTS):
        source = pieces.at[slot if c == AHEAD else other_side(slot), pl.ds(0, rows)]
        ins.append(pltpu.make_async_copy(source, held.at[slot], arrive.at[slot]))
        outs.append(pltpu.make_async_copy(held.at[slot], out.at[slot, place], leave.at[slot]))
    for copy in ins:
        copy.start()
    for slot in range(DECODE_SLOTS):
        ins[slot].wait()
        outs[slot].start()
    for copy in outs:
        copy.wait()


def stored_chunk(c, pieces, store):
    rows = CHUNKS[c] * BLOCK_TOKENS * HEADS
    operands = [pieces] + ([] if store is None else [store])
    anywhere = pl.BlockSpec(memory_space=pltpu.HBM)
    return pl.pallas_call(
        functools.partial(store_kernel, c),
        in_specs=[anywhere] * len(operands),
        out_specs=anywhere,
        out_shape=jax.ShapeDtypeStruct(
            (DECODE_SLOTS, 4 * BLOCK_TOKENS * HEADS, PAGE), jnp.bfloat16
        ),
        scratch_shapes=[
            pltpu.VMEM((DECODE_SLOTS, rows, PAGE), jnp.bfloat16),
            pltpu.SemaphoreType.DMA((DECODE_SLOTS,)),
            pltpu.SemaphoreType.DMA((DECODE_SLOTS,)),
        ],
        input_output_aliases={} if store is None else {1: 0},
        compiler_params=pltpu.CompilerParams(vmem_limit_bytes=VMEM),
        cost_estimate=LIGHT,
        name="stored_chunk",
    )(*operands)


def prefill_kernel(mask_ref, query_ref, cos_ref, sin_ref, *refs):
    page_ref = refs[0]
    out_ref, keys, values = refs[-3:]
    tokens = PROMPT_BLOCKS * BLOCK_TOKENS

    @pl.when(pl.program_id(0) == 0)
    def _():
        keys[:, :HEAD_SIZE] = page_ref[0, :, :HEAD_SIZE]
        values[:, :HEAD_SIZE] = page_ref[0, :, HEAD_SIZE:]
        block = lax.broadcasted_iota(jnp.int32, (tokens, HEAD_SIZE), 0) // BLOCK_TOKENS
        lane = lax.broadcasted_iota(jnp.int32, (tokens, HEAD_SIZE), 1)
        keys[:, HEAD_SIZE:] = jnp.where(block == lane, 1.0, 0.0).astype(jnp.bfloat16)
        values[:, HEAD_SIZE:] = jnp.ones((tokens, HEAD_SIZE), jnp.bfloat16)

    row = lax.broadcasted_iota(jnp.int32, (BLOCK_TOKENS, HEAD_SIZE), 0)
    column = lax.broadcasted_iota(jnp.int32, (BLOCK_TOKENS, HEAD_SIZE), 1)

    def masked_scores(head, first):
        lanes = slice(head * HEAD_SIZE, (head + 1) * HEAD_SIZE)
        rows = slice(first, first + QUERY_ROWS)
        blocks = range(first // BLOCK_TOKENS, (first + QUERY_ROWS) // BLOCK_TOKENS)
        width = PRE + -(-(first + QUERY_ROWS) // HEAD_SIZE) * HEAD_SIZE
        query = rotated(query_ref[rows, lanes], cos_ref[rows, :], sin_ref[rows, :])
        mask = jnp.concatenate(
            [
                jnp.broadcast_to(mask_ref[head, a : a + 1, :], (BLOCK_TOKENS, HEAD_SIZE))
                for a in blocks
            ],
            0,
        ).astype(jnp.bfloat16)
        scores = lax.dot_general(
            jnp.concatenate([query, mask], 1),
            keys[:width, :],
            (((1,), (1,)), ((), ())),
            preferred_element_type=jnp.float32,
        )
        parts = []
        for i, a in enumerate(blocks):
            part = scores[i * BLOCK_TOKENS : (i + 1) * BLOCK_TOKENS]
            start = PRE + a * BLOCK_TOKENS
            left = start // HEAD_SIZE * HEAD_SIZE
            right = left + HEAD_SIZE
            causal = column - (start - left) <= row
            pieces = [part[:, :left], jnp.where(causal, part[:, left:right], OFF)]
            if right < width:
                pieces.append(part[:, right:])
            parts.append(jnp.concatenate(pieces, 1))
        return jnp.concatenate(parts, 0)

    def attend(head, first, scores):
        peak = jnp.max(scores, axis=1, keepdims=True)
        weights = jnp.exp2((scores - peak) * EXP2_SCALE).astype(jnp.bfloat16)
        result = lax.dot_general(
            weights,
            values[: scores.shape[1], :],
            (((1,), (0,)), ((), ())),
            preferred_element_type=jnp.float32,
        )
        out_ref[first : first + QUERY_ROWS, head * HEAD_SIZE : (head + 1) * HEAD_SIZE] = (
            result[:, :HEAD_SIZE] / result[:, HEAD_SIZE:]
        ).astype(jnp.bfloat16)

    before = None
    for head in range(HEADS_AT_ONCE):
        for first in range(0, STRETCH_TOKENS, QUERY_ROWS):
            current = (head, first, masked_scores(head, first))
            if before is not None:
                attend(*before)
            before = current
    attend(*before)


def prefill_parts(part, count, mask, query, cos_part, sin_part, pages, out):
    tables = pl.BlockSpec((STRETCH_TOKENS, HEAD_SIZE), lambda i: (0, 0))
    prompt, half = divmod(part, PARTS)
    rows = pl.BlockSpec((STRETCH_TOKENS, HEADS_AT_ONCE * HEAD_SIZE), lambda i: (prompt, half + i))
    operands = [mask, query, cos_part, sin_part, pages] + ([] if out is None else [out])
    return pl.pallas_call(
        prefill_kernel,
        grid=(count,),
        in_specs=[
            pl.BlockSpec(
                (HEADS_AT_ONCE, STRETCH_BLOCKS, HEAD_SIZE), lambda i: (part + i, 0, 0)
            ),
            rows,
            tables,
            tables,
        ]
        + [pl.BlockSpec((1, PROMPT_BLOCKS * BLOCK_TOKENS, PAGE), lambda i: (prompt, 0, 0))]
        + ([] if out is None else [pl.BlockSpec(memory_space=pltpu.HBM)]),
        out_specs=rows,
        out_shape=jax.ShapeDtypeStruct(query.shape, query.dtype),
        scratch_shapes=[pltpu.VMEM((PROMPT_BLOCKS * BLOCK_TOKENS, PAGE), jnp.bfloat16)] * 2,
        input_output_aliases={} if out is None else {len(operands) - 1: 0},
        compiler_params=pltpu.CompilerParams(vmem_limit_bytes=VMEM),
        cost_estimate=LIGHT,
        name="prefill_parts",
    )(*operands)


def decode_kernel(length_ref, query_ref, fresh_ref, cos_ref, sin_ref, picked_ref, *refs):
    page_ref, outs = refs[0], refs[-N_TP:]
    prompt = pl.program_id(0)
    lines = DECODE_STEPS * HEADS
    tokens = PROMPT_BLOCKS * BLOCK_TOKENS
    width = tokens + HEAD_SIZE

    def by_step(array, rows, step):
        return jnp.where(step == 0, array[0:1], array[1:2])

    line = lax.broadcasted_iota(jnp.int32, (lines, HEAD_SIZE), 0)
    line_step = line % HEADS // (HEADS // 2)
    query = rotated(
        query_ref[0],
        by_step(cos_ref[0], lines, line_step),
        by_step(sin_ref[0], lines, line_step),
    )
    place = lax.broadcasted_iota(jnp.int32, (HEAD_SIZE, HEAD_SIZE), 0)
    fresh = fresh_ref[0].astype(jnp.float32)
    cos_part, sin_part = (by_step(r[0], HEAD_SIZE, place) for r in (cos_ref, sin_ref))
    fresh_keys = by_step(fresh[:, :HEAD_SIZE], HEAD_SIZE, place)
    fresh_keys = rotated(jnp.where(place < DECODE_STEPS, fresh_keys, 0.0), cos_part, sin_part)
    fresh_values = by_step(fresh[:, HEAD_SIZE:], HEAD_SIZE, place)
    fresh_values = jnp.where(place < DECODE_STEPS, fresh_values, 0.0).astype(jnp.bfloat16)
    keys = jnp.concatenate([page_ref[0, :, :HEAD_SIZE], fresh_keys], 0)
    values = jnp.concatenate([page_ref[0, :, HEAD_SIZE:], fresh_values], 0)
    scores = lax.dot_general(
        query, keys, (((1,), (1,)), ((), ())), preferred_element_type=jnp.float32
    )
    number = lax.broadcasted_iota(jnp.int32, (lines, width), 1)
    block = number // BLOCK_TOKENS
    step = lax.broadcasted_iota(jnp.int32, (lines, width), 0) % HEADS // (HEADS // 2)
    picked = picked_ref[0]
    kept = block >= NBP
    for i in range(SELECTED_BLOCKS):
        kept = kept | (picked[:, i : i + 1] == block)
    kept = kept & (number < length_ref[prompt])
    kept = (kept & (number < tokens)) | ((number >= tokens) & (number - tokens <= step))
    scores = jnp.where(kept, scores, OFF)
    peak = jnp.max(scores, axis=1, keepdims=True)
    weights = jnp.where(kept, jnp.exp2((scores - peak) * EXP2_SCALE), 0.0)
    total = jnp.sum(weights, axis=1, keepdims=True)
    coarse = weights.astype(jnp.bfloat16)
    fine = (weights - coarse.astype(jnp.float32)).astype(jnp.bfloat16)
    result = lax.dot_general(
        jnp.concatenate([coarse, fine], 0),
        values,
        (((1,), (0,)), ((), ())),
        preferred_element_type=jnp.float32,
    )
    result = (result[:lines] + result[lines:]) / total
    result = jnp.concatenate([result[:HEADS], result[HEADS:]], 1)
    result = jnp.concatenate([result, jnp.zeros_like(result)], 0).astype(jnp.bfloat16)
    for out in outs:
        out[0] = result


def decoded(lengths, query, fresh, cos_part, sin_part, picked, pages, leaving):
    def one(array):
        return pl.BlockSpec((1,) + array.shape[1:], lambda n, *_: (n, 0, 0))

    operands = [query, fresh, cos_part, sin_part, picked, pages]
    place = CHUNKS[LAST] * BLOCK_TOKENS // RESULT_ROWS
    return pl.pallas_call(
        decode_kernel,
        grid_spec=pltpu.PrefetchScalarGridSpec(
            num_scalar_prefetch=1,
            grid=(REQ_DEV,),
            in_specs=[one(x) for x in operands] + [pl.BlockSpec(memory_space=pltpu.HBM)] * N_TP,
            out_specs=[pl.BlockSpec((1, RESULT_ROWS, PAGE), lambda n, *_: (n, place, 0))] * N_TP,
        ),
        out_shape=[jax.ShapeDtypeStruct(x.shape, jnp.bfloat16) for x in leaving],
        input_output_aliases={1 + len(operands) + j: j for j in range(N_TP)},
        compiler_params=pltpu.CompilerParams(vmem_limit_bytes=VMEM),
        cost_estimate=LIGHT,
        name="decoded",
    )(lengths, *operands, *leaving)


def after(array, *others):
    return lax.optimization_barrier((array, *others))[0]


def shards(
    stretch_query,
    stretch_kv,
    prefix_page_store,
    page_table,
    vs_mask,
    prompt_lengths,
    placement,
    step_query_rows,
    step_key_value,
    selected_prefix_blocks,
):
    axes = ("section", "req", "tp")
    section = lax.axis_index("section")
    req = lax.axis_index("req")
    tp = lax.axis_index("tp")

    def across(leaving):
        return [
            lax.ppermute(pages, axes, cross_route(offset))
            for pages, offset in zip(leaving, TP_OFFSETS)
        ]

    own_heads = HEADS * HEAD_SIZE
    queries = lax.dynamic_slice_in_dim(step_query_rows[0], tp * own_heads, own_heads, 2)
    fresh = lax.dynamic_index_in_dim(step_key_value[0], tp, 2, keepdims=False)
    picks = lax.dynamic_slice_in_dim(selected_prefix_blocks[0], tp * HEADS, HEADS, 2)
    load = jnp.concatenate(
        [queries, fresh, picks.astype(jnp.bfloat16).reshape(DECODE_SLOTS, DECODE_STEPS, -1)],
        axis=-1,
    )
    sections = jnp.arange(2, dtype=jnp.int32)[:, None, None, None]
    load = jnp.where(sections == 1 - section, load[None], jnp.zeros((), load.dtype))
    sent = load
    load = lax.all_to_all(
        load.reshape((2 * N_REQ,) + load.shape[2:]),
        ("section", "req"),
        split_axis=0,
        concat_axis=0,
        tiled=True,
    )

    cos_part, sin_part = rope_tables(PRE + jnp.arange(STRETCH_TOKENS, dtype=jnp.int32))
    tp_targets = jnp.stack([tp_moved(tp, offset) for offset in TP_OFFSETS]).astype(jnp.int32)
    pages, leaving, ahead = assembled(
        tp_targets,
        after(page_table, sent),
        prefix_page_store.reshape(PREFIX_PAGES, BLOCK_TOKENS, PAGE),
        stretch_kv.reshape(-1, PAGE),
        cos_part,
        sin_part,
    )
    ahead = lax.all_to_all(after(ahead, load), "tp", split_axis=0, concat_axis=0, tiled=True)
    arrived = [across(chunk) for chunk in leaving[:LAST]]

    mask = jnp.where(vs_mask == 1, 0.0, OFF).reshape(-1, STRETCH_BLOCKS, PROMPT_BLOCKS)
    mask = jnp.pad(mask, ((0, 0), (0, 0), (0, HEAD_SIZE - PROMPT_BLOCKS)))

    def prefilled(part, count, out, *others):
        return prefill_parts(
            part, count, after(mask, *others), stretch_query, cos_part, sin_part, pages, out
        )

    own_row = section * N_REQ + req
    targets = lax.dynamic_index_in_dim(placement, own_row, 0, keepdims=False)
    load = jnp.take(load, (1 - section) * N_REQ + targets, axis=0)
    lengths = PRE + lax.dynamic_slice_in_dim(prompt_lengths, own_row * REQ_DEV, REQ_DEV, 0)
    steps = jnp.arange(DECODE_STEPS, dtype=jnp.int32)
    step_cos, step_sin = rope_tables(lengths[:, None] + steps)

    def by_line(array):
        array = array.reshape(REQ_DEV, DECODE_STEPS, HEADS // 2, 2, -1)
        return jnp.transpose(array, (0, 3, 1, 2, 4)).reshape(REQ_DEV, DECODE_STEPS * HEADS, -1)

    origin = (1 - section) * N_REQ + other_side(req)
    origin_targets = lax.dynamic_index_in_dim(placement, origin, 0, keepdims=False)
    number = jnp.arange(REQ_DEV, dtype=jnp.int32)
    group = jnp.arange(N_REQ, dtype=jnp.int32)

    def prompt_for(targets):
        return jnp.max(jnp.where(targets == group[:, None], number, -1), axis=-1)

    prompts = prompt_for(origin_targets)
    lines = other_side(targets)

    def over_req(pages):
        return lax.all_to_all(pages, "req", split_axis=0, concat_axis=0, tiled=True)

    heads = jnp.stack([tp_moved(tp, offset, -1) for offset in TP_OFFSETS]).astype(jnp.int32)
    prefill_out = None
    waiting, gone = {}, {}
    store = None
    before = None
    for step in ORDER:
        step, _, piece = step.partition("@")
        kind, n = step[0], int(step[1:] or 0)
        others = () if before is None else (before,)
        if piece:
            if piece in gone:
                others += (gone[piece],)
            else:
                others += tuple(arrived[int(piece[0])][: int(piece[1]) + 1])
        if kind == "d":
            full_last = decoded(
                after(lengths, *others),
                by_line(load[..., :own_heads]),
                load[..., own_heads : own_heads + PAGE],
                step_cos,
                step_sin,
                by_line(load[..., own_heads + PAGE :]).astype(jnp.int32),
                pages,
                leaving[LAST],
            )
            arrived.append(across(full_last))
            before = full_last[0]
        elif kind == "r":
            chunk = list(arrived[n])
            chunk[0] = after(chunk[0], *others)
            before = routed_pages(n, origin_targets, prompts, heads, chunk)
            waiting[n] = gone[str(n)] = over_req(before)
        elif kind == "a":
            before = routed_pages(AHEAD, lines, prompt_for(lines), group, [after(ahead, *others)])
            gone["a"] = over_req(before)
            waiting[AHEAD] = lax.ppermute(gone["a"], axes, cross_route(TP_OFFSETS[0]))
            gone["x"] = waiting[AHEAD]
        elif kind == "p":
            before = prefill_out = prefilled(n, 1, prefill_out, *others)
        elif kind == "P":
            before = prefill_out = prefilled(n * PARTS, PARTS, prefill_out, *others)
        else:
            before = store = stored_chunk(n, after(waiting[n], *others), store)
    routed = waiting[LAST]
    store = store.reshape(1, DECODE_SLOTS, 4, BLOCK_TOKENS, KEY_VALUE_HEADS, PAGE)
    first = CHUNKS[LAST] * BLOCK_TOKENS * HEADS
    results = routed[:, first : first + HEADS * KEY_VALUE_HEADS]
    results = results.reshape(2, N_REQ // 2, DECODE_STEPS, HEADS // 2, KEY_VALUE_HEADS, PAGE)
    results = jnp.transpose(results[::-1], (0, 1, 2, 4, 3, 5))
    decode_output = results.reshape(1, DECODE_SLOTS, DECODE_STEPS, QUERY_HEADS * HEAD_SIZE)
    return (prefill_out, store, decode_output)


def solution(mesh):
    placed = (
        P(("section", "req"), "tp"),
        P(("section", "req"), "tp", None),
        P(("section", "req"), None, "tp", None),
        P(("section", "req"), None),
        P(("section", "req"), "tp", None, None),
        P(),
        P(),
        P(("section", "req"), None, None, None),
        P(("section", "req"), None, None, None, None),
        P(("section", "req"), None, None, None, None),
    )
    return jax.shard_map(
        shards,
        mesh=mesh,
        in_specs=placed,
        out_specs=(
            P(("section", "req"), "tp"),
            P(("section", "req"), None, "tp", None, None, None),
            P(("section", "req"), None, None, None),
        ),
        check_vma=False,
    )
```

```python
import functools
import math

import jax
import jax.numpy as jnp
from jax import lax
from jax.experimental import pallas as pl
from jax.experimental.pallas import tpu as pltpu
from jax.sharding import PartitionSpec as P

QUERY_HEADS = 64
KEY_VALUE_HEADS = 8
HEAD_SIZE = 128
PRE = 1536
STRETCH_TOKENS = 512
BLOCK_TOKENS = 64
REQ_DEV = 4
DECODE_STEPS = 2
DECODE_SLOTS = 8
NBP = 24
STRETCH_BLOCKS = 8
PROMPT_BLOCKS = 32
SELECTED_BLOCKS = 8
PREFIX_PAGES = 96
HEADS = 8
PAGE = 2 * HEAD_SIZE
N_TP = 8
N_REQ = 8
RESULT_ROWS = 16
CHUNKS = (2, 1, 1)
LAST = 1
AHEAD = 2
STARTS = tuple(sum(CHUNKS[:c]) for c in range(len(CHUNKS)))
HEADS_AT_ONCE = 4
ORDER = ('a@01', 'd', 'p0@05', 'r0', 'p1@10', 'P1', 'r1', 'P2', 's0', 'P3', 's2@x', 's1')
QUERY_ROWS = 256
PARTS = HEADS // HEADS_AT_ONCE

ROPE_BASE = 500000.0
OFF = -1e30
EXP2_SCALE = math.log2(math.e) / math.sqrt(HEAD_SIZE)
VMEM = 60 << 20
LIGHT = pl.CostEstimate(flops=1, bytes_accessed=1, transcendentals=0)

def all_places():
    for section in range(2):
        for req in range(N_REQ):
            for tp in range(N_TP):
                yield section, req, tp


def place_number(section, req, tp):
    return (section * N_REQ + req) * N_TP + tp


def other_side(req):
    return (req + N_REQ // 2) % N_REQ


TP_OFFSETS = [(dz, dc) for dz in range(4) for dc in range(2)]


def tp_moved(tp, offset, sign=1):
    dz, dc = offset
    return (tp // 2 + sign * dz + 4) % 4 * 2 + (tp + dc) % 2


def cross_route(offset):
    return [
        (place_number(s, r, t), place_number(1 - s, other_side(r), tp_moved(t, offset)))
        for s, r, t in all_places()
    ]


def routed_rows(c):
    extra = DECODE_STEPS * HEADS // 2 if c == LAST else 0
    return (CHUNKS[c] * BLOCK_TOKENS + extra) * HEADS


def travelling_rows(c):
    return CHUNKS[c] * BLOCK_TOKENS + (RESULT_ROWS if c == LAST else 0)


def rope_tables(positions):
    half = HEAD_SIZE // 2
    frequency = jnp.exp(
        -math.log(ROPE_BASE) * (2.0 * jnp.arange(half, dtype=jnp.float32) / HEAD_SIZE)
    )
    angles = positions.astype(jnp.float32)[..., None] * frequency
    cos_part, sin_part = jnp.cos(angles), jnp.sin(angles)
    return (
        jnp.concatenate([cos_part, cos_part], -1),
        jnp.concatenate([-sin_part, sin_part], -1),
    )


def rotated(rows, cos_part, sin_part):
    rows = rows.astype(jnp.float32)
    return (rows * cos_part + pltpu.roll(rows, HEAD_SIZE // 2, 1) * sin_part).astype(jnp.bfloat16)


def assemble_kernel(target_ref, table_ref, prefix_ref, kv_ref, cos_ref, sin_ref, *refs):
    chunks = range(len(CHUNKS))
    own, outs, (held, arrive, leave) = refs[0], refs[1:-3], refs[-3:]
    copies = [[] for _ in chunks]
    for c, count in enumerate(CHUNKS):
        for target in range(NBP // 4):
            for prompt in range(REQ_DEV):
                for b in range(count):
                    block = target * 4 + STARTS[c] + b
                    place = held.at[prompt, pl.ds(block * BLOCK_TOKENS, BLOCK_TOKENS)]
                    page = table_ref[prompt, block]
                    copies[c].append(
                        pltpu.make_async_copy(prefix_ref.at[page], place, arrive.at[c])
                    )
                    copies[c][-1].start()
    for prompt in range(REQ_DEV):
        rows = slice(prompt * STRETCH_TOKENS, (prompt + 1) * STRETCH_TOKENS)
        held[prompt, PRE:, :HEAD_SIZE] = rotated(
            kv_ref[rows, :HEAD_SIZE], cos_ref[...], sin_ref[...]
        )
        held[prompt, PRE:, HEAD_SIZE:] = kv_ref[rows, HEAD_SIZE:]
    out_copies = []
    for c, count in enumerate(CHUNKS):
        size = count * BLOCK_TOKENS
        for copy in copies[c]:
            copy.wait()
        for j in range(N_TP):
            target = j if c == AHEAD else target_ref[j]
            first = (target * 4 + STARTS[c]) * BLOCK_TOKENS
            if c != AHEAD:
                first = pl.multiple_of(first, BLOCK_TOKENS)
            out_copies.append(
                pltpu.make_async_copy(
                    held.at[:, pl.ds(first, size)],
                    outs[-1].at[j] if c == AHEAD else outs[c * N_TP + j].at[:, pl.ds(0, size)],
                    leave.at[c],
                )
            )
            out_copies[-1].start()
    out_copies.append(pltpu.make_async_copy(held, own, leave.at[len(CHUNKS)]))
    out_copies[-1].start()
    for copy in out_copies:
        copy.wait()


def assembled(targets, table, prefix, kv, cos_part, sin_part):
    anywhere = pl.BlockSpec(memory_space=pltpu.HBM)
    whole = pl.BlockSpec(memory_space=pltpu.VMEM)
    scalars = pl.BlockSpec(memory_space=pltpu.SMEM)
    own = (REQ_DEV, PROMPT_BLOCKS * BLOCK_TOKENS, PAGE)
    shapes = [own] + [
        (REQ_DEV, travelling_rows(c), PAGE) for c in range(AHEAD) for _ in range(N_TP)
    ]
    shapes.append((N_TP, REQ_DEV, travelling_rows(AHEAD), PAGE))
    outs = pl.pallas_call(
        assemble_kernel,
        in_specs=[scalars, scalars, anywhere, whole, whole, whole],
        out_specs=[anywhere] * len(shapes),
        out_shape=[jax.ShapeDtypeStruct(shape, jnp.bfloat16) for shape in shapes],
        scratch_shapes=[
            pltpu.VMEM(own, jnp.bfloat16),
            pltpu.SemaphoreType.DMA((len(CHUNKS),)),
            pltpu.SemaphoreType.DMA((len(CHUNKS) + 1,)),
        ],
        compiler_params=pltpu.CompilerParams(vmem_limit_bytes=VMEM),
        cost_estimate=LIGHT,
        name="assembled",
    )(targets, table, prefix, kv, cos_part, sin_part)
    chunks = [outs[1 + c * N_TP : 1 + (c + 1) * N_TP] for c in range(AHEAD)]
    return outs[0], chunks, outs[-1]


def route_kernel(width, group_ref, prompt_ref, head_ref, *refs):
    arrived, (out, spread, packed, empty, sem) = refs[:-5], refs[-5:]
    prompt = pl.program_id(0)
    rows = width // HEADS

    @pl.when(prompt == 0)
    def _():
        empty[...] = jnp.zeros_like(empty)
        for d in range(N_REQ):

            @pl.when(prompt_ref[d] < 0)
            def _():
                pltpu.make_async_copy(empty, out.at[d], sem).start()

    for first in range(0, rows, BLOCK_TOKENS):
        size = min(BLOCK_TOKENS, rows - first)
        for half in range(2):
            lanes = pl.ds(half * HEAD_SIZE, HEAD_SIZE)
            for j in range(N_TP):
                part = pl.ds(first, max(size, RESULT_ROWS))
                if len(arrived) == 1:
                    block = arrived[0][j, 0, part, lanes]
                else:
                    block = arrived[j][0, part, lanes]
                places = pl.ds(first * HEADS + head_ref[j], size, stride=HEADS)
                spread[half, places, :] = block.astype(jnp.float32)[:size]
            part = pl.ds(first * HEADS, size * HEADS)
            packed[prompt, part, lanes] = spread[half, part, :].astype(jnp.bfloat16)
    pltpu.make_async_copy(packed.at[prompt], out.at[group_ref[prompt]], sem).start()

    @pl.when(prompt == REQ_DEV - 1)
    def _():
        pltpu.make_async_copy(out, out, sem).wait()


def routed_pages(c, targets, prompts, heads, arrived):
    rows, width = travelling_rows(c), routed_rows(c)
    return pl.pallas_call(
        functools.partial(route_kernel, width),
        grid_spec=pltpu.PrefetchScalarGridSpec(
            num_scalar_prefetch=3,
            grid=(REQ_DEV,),
            in_specs=[pl.BlockSpec((N_TP, 1, rows, PAGE), lambda n, *_: (0, n, 0, 0))]
            if c == AHEAD
            else [pl.BlockSpec((1, rows, PAGE), lambda n, *_: (n, 0, 0))] * N_TP,
            out_specs=pl.BlockSpec(memory_space=pltpu.HBM),
            scratch_shapes=[
                pltpu.VMEM((2, width, HEAD_SIZE), jnp.float32),
                pltpu.VMEM((REQ_DEV, width, PAGE), jnp.bfloat16),
                pltpu.VMEM((width, PAGE), jnp.bfloat16),
                pltpu.SemaphoreType.DMA,
            ],
        ),
        out_shape=jax.ShapeDtypeStruct((N_REQ, width, PAGE), jnp.bfloat16),
        compiler_params=pltpu.CompilerParams(vmem_limit_bytes=VMEM),
        cost_estimate=LIGHT,
        name="routed_pages",
    )(targets, prompts, heads, *arrived)


def store_kernel(c, pieces, *refs):
    out, held, arrive, leave = refs[-4:]
    rows = CHUNKS[c] * BLOCK_TOKENS * HEADS
    place = pl.ds(STARTS[c] * BLOCK_TOKENS * HEADS, rows)
    ins, outs = [], []
    for slot in range(DECODE_SLOTS):
        source = pieces.at[slot if c == AHEAD else other_side(slot), pl.ds(0, rows)]
        ins.append(pltpu.make_async_copy(source, held.at[slot], arrive.at[slot]))
        outs.append(pltpu.make_async_copy(held.at[slot], out.at[slot, place], leave.at[slot]))
    for copy in ins:
        copy.start()
    for slot in range(DECODE_SLOTS):
        ins[slot].wait()
        outs[slot].start()
    for copy in outs:
        copy.wait()


def stored_chunk(c, pieces, store):
    rows = CHUNKS[c] * BLOCK_TOKENS * HEADS
    operands = [pieces] + ([] if store is None else [store])
    anywhere = pl.BlockSpec(memory_space=pltpu.HBM)
    return pl.pallas_call(
        functools.partial(store_kernel, c),
        in_specs=[anywhere] * len(operands),
        out_specs=anywhere,
        out_shape=jax.ShapeDtypeStruct(
            (DECODE_SLOTS, 4 * BLOCK_TOKENS * HEADS, PAGE), jnp.bfloat16
        ),
        scratch_shapes=[
            pltpu.VMEM((DECODE_SLOTS, rows, PAGE), jnp.bfloat16),
            pltpu.SemaphoreType.DMA((DECODE_SLOTS,)),
            pltpu.SemaphoreType.DMA((DECODE_SLOTS,)),
        ],
        input_output_aliases={} if store is None else {1: 0},
        compiler_params=pltpu.CompilerParams(vmem_limit_bytes=VMEM),
        cost_estimate=LIGHT,
        name="stored_chunk",
    )(*operands)


def prefill_kernel(mask_ref, query_ref, cos_ref, sin_ref, *refs):
    page_ref = refs[0]
    out_ref, keys, values = refs[-3:]
    tokens = PROMPT_BLOCKS * BLOCK_TOKENS

    @pl.when(pl.program_id(0) == 0)
    def _():
        keys[:, :HEAD_SIZE] = page_ref[0, :, :HEAD_SIZE]
        values[:, :HEAD_SIZE] = page_ref[0, :, HEAD_SIZE:]
        block = lax.broadcasted_iota(jnp.int32, (tokens, HEAD_SIZE), 0) // BLOCK_TOKENS
        lane = lax.broadcasted_iota(jnp.int32, (tokens, HEAD_SIZE), 1)
        keys[:, HEAD_SIZE:] = jnp.where(block == lane, 1.0, 0.0).astype(jnp.bfloat16)
        values[:, HEAD_SIZE:] = jnp.ones((tokens, HEAD_SIZE), jnp.bfloat16)

    row = lax.broadcasted_iota(jnp.int32, (BLOCK_TOKENS, HEAD_SIZE), 0)
    column = lax.broadcasted_iota(jnp.int32, (BLOCK_TOKENS, HEAD_SIZE), 1)

    def masked_scores(head, first):
        lanes = slice(head * HEAD_SIZE, (head + 1) * HEAD_SIZE)
        rows = slice(first, first + QUERY_ROWS)
        blocks = range(first // BLOCK_TOKENS, (first + QUERY_ROWS) // BLOCK_TOKENS)
        width = PRE + -(-(first + QUERY_ROWS) // HEAD_SIZE) * HEAD_SIZE
        query = rotated(query_ref[rows, lanes], cos_ref[rows, :], sin_ref[rows, :])
        mask = jnp.concatenate(
            [
                jnp.broadcast_to(mask_ref[head, a : a + 1, :], (BLOCK_TOKENS, HEAD_SIZE))
                for a in blocks
            ],
            0,
        ).astype(jnp.bfloat16)
        scores = lax.dot_general(
            jnp.concatenate([query, mask], 1),
            keys[:width, :],
            (((1,), (1,)), ((), ())),
            preferred_element_type=jnp.float32,
        )
        parts = []
        for i, a in enumerate(blocks):
            part = scores[i * BLOCK_TOKENS : (i + 1) * BLOCK_TOKENS]
            start = PRE + a * BLOCK_TOKENS
            left = start // HEAD_SIZE * HEAD_SIZE
            right = left + HEAD_SIZE
            causal = column - (start - left) <= row
            pieces = [part[:, :left], jnp.where(causal, part[:, left:right], OFF)]
            if right < width:
                pieces.append(part[:, right:])
            parts.append(jnp.concatenate(pieces, 1))
        return jnp.concatenate(parts, 0)

    def attend(head, first, scores):
        peak = jnp.max(scores, axis=1, keepdims=True)
        weights = jnp.exp2((scores - peak) * EXP2_SCALE).astype(jnp.bfloat16)
        result = lax.dot_general(
            weights,
            values[: scores.shape[1], :],
            (((1,), (0,)), ((), ())),
            preferred_element_type=jnp.float32,
        )
        out_ref[first : first + QUERY_ROWS, head * HEAD_SIZE : (head + 1) * HEAD_SIZE] = (
            result[:, :HEAD_SIZE] / result[:, HEAD_SIZE:]
        ).astype(jnp.bfloat16)

    before = None
    for head in range(HEADS_AT_ONCE):
        for first in range(0, STRETCH_TOKENS, QUERY_ROWS):
            current = (head, first, masked_scores(head, first))
            if before is not None:
                attend(*before)
            before = current
    attend(*before)


def prefill_parts(part, count, mask, query, cos_part, sin_part, pages, out):
    tables = pl.BlockSpec((STRETCH_TOKENS, HEAD_SIZE), lambda i: (0, 0))
    prompt, half = divmod(part, PARTS)
    rows = pl.BlockSpec((STRETCH_TOKENS, HEADS_AT_ONCE * HEAD_SIZE), lambda i: (prompt, half + i))
    operands = [mask, query, cos_part, sin_part, pages] + ([] if out is None else [out])
    return pl.pallas_call(
        prefill_kernel,
        grid=(count,),
        in_specs=[
            pl.BlockSpec(
                (HEADS_AT_ONCE, STRETCH_BLOCKS, HEAD_SIZE), lambda i: (part + i, 0, 0)
            ),
            rows,
            tables,
            tables,
        ]
        + [pl.BlockSpec((1, PROMPT_BLOCKS * BLOCK_TOKENS, PAGE), lambda i: (prompt, 0, 0))]
        + ([] if out is None else [pl.BlockSpec(memory_space=pltpu.HBM)]),
        out_specs=rows,
        out_shape=jax.ShapeDtypeStruct(query.shape, query.dtype),
        scratch_shapes=[pltpu.VMEM((PROMPT_BLOCKS * BLOCK_TOKENS, PAGE), jnp.bfloat16)] * 2,
        input_output_aliases={} if out is None else {len(operands) - 1: 0},
        compiler_params=pltpu.CompilerParams(vmem_limit_bytes=VMEM),
        cost_estimate=LIGHT,
        name="prefill_parts",
    )(*operands)


def decode_kernel(length_ref, query_ref, fresh_ref, cos_ref, sin_ref, picked_ref, *refs):
    page_ref, outs = refs[0], refs[-N_TP:]
    prompt = pl.program_id(0)
    lines = DECODE_STEPS * HEADS
    tokens = PROMPT_BLOCKS * BLOCK_TOKENS
    width = tokens + HEAD_SIZE

    def by_step(array, rows, step):
        return jnp.where(step == 0, array[0:1], array[1:2])

    line = lax.broadcasted_iota(jnp.int32, (lines, HEAD_SIZE), 0)
    line_step = line % HEADS // (HEADS // 2)
    query = rotated(
        query_ref[0],
        by_step(cos_ref[0], lines, line_step),
        by_step(sin_ref[0], lines, line_step),
    )
    place = lax.broadcasted_iota(jnp.int32, (HEAD_SIZE, HEAD_SIZE), 0)
    fresh = fresh_ref[0].astype(jnp.float32)
    cos_part, sin_part = (by_step(r[0], HEAD_SIZE, place) for r in (cos_ref, sin_ref))
    fresh_keys = by_step(fresh[:, :HEAD_SIZE], HEAD_SIZE, place)
    fresh_keys = rotated(jnp.where(place < DECODE_STEPS, fresh_keys, 0.0), cos_part, sin_part)
    fresh_values = by_step(fresh[:, HEAD_SIZE:], HEAD_SIZE, place)
    fresh_values = jnp.where(place < DECODE_STEPS, fresh_values, 0.0).astype(jnp.bfloat16)
    keys = jnp.concatenate([page_ref[0, :, :HEAD_SIZE], fresh_keys], 0)
    values = jnp.concatenate([page_ref[0, :, HEAD_SIZE:], fresh_values], 0)
    scores = lax.dot_general(
        query, keys, (((1,), (1,)), ((), ())), preferred_element_type=jnp.float32
    )
    number = lax.broadcasted_iota(jnp.int32, (lines, width), 1)
    block = number // BLOCK_TOKENS
    step = lax.broadcasted_iota(jnp.int32, (lines, width), 0) % HEADS // (HEADS // 2)
    picked = picked_ref[0]
    kept = block >= NBP
    for i in range(SELECTED_BLOCKS):
        kept = kept | (picked[:, i : i + 1] == block)
    kept = kept & (number < length_ref[prompt])
    kept = (kept & (number < tokens)) | ((number >= tokens) & (number - tokens <= step))
    scores = jnp.where(kept, scores, OFF)
    peak = jnp.max(scores, axis=1, keepdims=True)
    weights = jnp.where(kept, jnp.exp2((scores - peak) * EXP2_SCALE), 0.0)
    total = jnp.sum(weights, axis=1, keepdims=True)
    coarse = weights.astype(jnp.bfloat16)
    fine = (weights - coarse.astype(jnp.float32)).astype(jnp.bfloat16)
    result = lax.dot_general(
        jnp.concatenate([coarse, fine], 0),
        values,
        (((1,), (0,)), ((), ())),
        preferred_element_type=jnp.float32,
    )
    result = (result[:lines] + result[lines:]) / total
    result = jnp.concatenate([result[:HEADS], result[HEADS:]], 1)
    result = jnp.concatenate([result, jnp.zeros_like(result)], 0).astype(jnp.bfloat16)
    for out in outs:
        out[0] = result


def decoded(lengths, query, fresh, cos_part, sin_part, picked, pages, leaving):
    def one(array):
        return pl.BlockSpec((1,) + array.shape[1:], lambda n, *_: (n, 0, 0))

    operands = [query, fresh, cos_part, sin_part, picked, pages]
    place = CHUNKS[LAST] * BLOCK_TOKENS // RESULT_ROWS
    return pl.pallas_call(
        decode_kernel,
        grid_spec=pltpu.PrefetchScalarGridSpec(
            num_scalar_prefetch=1,
            grid=(REQ_DEV,),
            in_specs=[one(x) for x in operands] + [pl.BlockSpec(memory_space=pltpu.HBM)] * N_TP,
            out_specs=[pl.BlockSpec((1, RESULT_ROWS, PAGE), lambda n, *_: (n, place, 0))] * N_TP,
        ),
        out_shape=[jax.ShapeDtypeStruct(x.shape, jnp.bfloat16) for x in leaving],
        input_output_aliases={1 + len(operands) + j: j for j in range(N_TP)},
        compiler_params=pltpu.CompilerParams(vmem_limit_bytes=VMEM),
        cost_estimate=LIGHT,
        name="decoded",
    )(lengths, *operands, *leaving)


def after(array, *others):
    return lax.optimization_barrier((array, *others))[0]


def shards(
    stretch_query,
    stretch_kv,
    prefix_page_store,
    page_table,
    vs_mask,
    prompt_lengths,
    placement,
    step_query_rows,
    step_key_value,
    selected_prefix_blocks,
):
    axes = ("section", "req", "tp")
    section = lax.axis_index("section")
    req = lax.axis_index("req")
    tp = lax.axis_index("tp")

    def across(leaving):
        return [
            lax.ppermute(pages, axes, cross_route(offset))
            for pages, offset in zip(leaving, TP_OFFSETS)
        ]

    own_heads = HEADS * HEAD_SIZE
    queries = lax.dynamic_slice_in_dim(step_query_rows[0], tp * own_heads, own_heads, 2)
    fresh = lax.dynamic_index_in_dim(step_key_value[0], tp, 2, keepdims=False)
    picks = lax.dynamic_slice_in_dim(selected_prefix_blocks[0], tp * HEADS, HEADS, 2)
    load = jnp.concatenate(
        [queries, fresh, picks.astype(jnp.bfloat16).reshape(DECODE_SLOTS, DECODE_STEPS, -1)],
        axis=-1,
    )
    sections = jnp.arange(2, dtype=jnp.int32)[:, None, None, None]
    load = jnp.where(sections == 1 - section, load[None], jnp.zeros((), load.dtype))
    sent = load
    load = lax.all_to_all(
        load.reshape((2 * N_REQ,) + load.shape[2:]),
        ("section", "req"),
        split_axis=0,
        concat_axis=0,
        tiled=True,
    )

    cos_part, sin_part = rope_tables(PRE + jnp.arange(STRETCH_TOKENS, dtype=jnp.int32))
    tp_targets = jnp.stack([tp_moved(tp, offset) for offset in TP_OFFSETS]).astype(jnp.int32)
    pages, leaving, ahead = assembled(
        tp_targets,
        after(page_table, sent),
        prefix_page_store.reshape(PREFIX_PAGES, BLOCK_TOKENS, PAGE),
        stretch_kv.reshape(-1, PAGE),
        cos_part,
        sin_part,
    )
    ahead = lax.all_to_all(after(ahead, load), "tp", split_axis=0, concat_axis=0, tiled=True)
    arrived = [across(chunk) for chunk in leaving[:LAST]]

    mask = jnp.where(vs_mask == 1, 0.0, OFF).reshape(-1, STRETCH_BLOCKS, PROMPT_BLOCKS)
    mask = jnp.pad(mask, ((0, 0), (0, 0), (0, HEAD_SIZE - PROMPT_BLOCKS)))

    def prefilled(part, count, out, *others):
        return prefill_parts(
            part, count, after(mask, *others), stretch_query, cos_part, sin_part, pages, out
        )

    own_row = section * N_REQ + req
    targets = lax.dynamic_index_in_dim(placement, own_row, 0, keepdims=False)
    load = jnp.take(load, (1 - section) * N_REQ + targets, axis=0)
    lengths = PRE + lax.dynamic_slice_in_dim(prompt_lengths, own_row * REQ_DEV, REQ_DEV, 0)
    steps = jnp.arange(DECODE_STEPS, dtype=jnp.int32)
    step_cos, step_sin = rope_tables(lengths[:, None] + steps)

    def by_line(array):
        array = array.reshape(REQ_DEV, DECODE_STEPS, HEADS // 2, 2, -1)
        return jnp.transpose(array, (0, 3, 1, 2, 4)).reshape(REQ_DEV, DECODE_STEPS * HEADS, -1)

    origin = (1 - section) * N_REQ + other_side(req)
    origin_targets = lax.dynamic_index_in_dim(placement, origin, 0, keepdims=False)
    number = jnp.arange(REQ_DEV, dtype=jnp.int32)
    group = jnp.arange(N_REQ, dtype=jnp.int32)

    def prompt_for(targets):
        return jnp.max(jnp.where(targets == group[:, None], number, -1), axis=-1)

    prompts = prompt_for(origin_targets)
    lines = other_side(targets)

    def over_req(pages):
        return lax.all_to_all(pages, "req", split_axis=0, concat_axis=0, tiled=True)

    heads = jnp.stack([tp_moved(tp, offset, -1) for offset in TP_OFFSETS]).astype(jnp.int32)
    prefill_out = None
    waiting, gone = {}, {}
    store = None
    before = None
    for step in ORDER:
        step, _, piece = step.partition("@")
        kind, n = step[0], int(step[1:] or 0)
        others = () if before is None else (before,)
        if piece:
            if piece in gone:
                others += (gone[piece],)
            else:
                others += tuple(arrived[int(piece[0])][: int(piece[1]) + 1])
        if kind == "d":
            full_last = decoded(
                after(lengths, *others),
                by_line(load[..., :own_heads]),
                load[..., own_heads : own_heads + PAGE],
                step_cos,
                step_sin,
                by_line(load[..., own_heads + PAGE :]).astype(jnp.int32),
                pages,
                leaving[LAST],
            )
            arrived.append(across(full_last))
            before = full_last[0]
        elif kind == "r":
            chunk = list(arrived[n])
            chunk[0] = after(chunk[0], *others)
            before = routed_pages(n, origin_targets, prompts, heads, chunk)
            earlier = gone["a" if n == 0 else str(n - 1)]
            waiting[n] = gone[str(n)] = over_req(after(before, earlier))
        elif kind == "a":
            before = routed_pages(AHEAD, lines, prompt_for(lines), group, [after(ahead, *others)])
            gone["a"] = over_req(before)
            waiting[AHEAD] = lax.ppermute(gone["a"], axes, cross_route(TP_OFFSETS[0]))
            gone["x"] = waiting[AHEAD]
        elif kind == "p":
            before = prefill_out = prefilled(n, 1, prefill_out, *others)
        elif kind == "P":
            before = prefill_out = prefilled(n * PARTS, PARTS, prefill_out, *others)
        else:
            before = store = stored_chunk(n, after(waiting[n], *others), store)
    routed = waiting[LAST]
    store = store.reshape(1, DECODE_SLOTS, 4, BLOCK_TOKENS, KEY_VALUE_HEADS, PAGE)
    first = CHUNKS[LAST] * BLOCK_TOKENS * HEADS
    results = routed[:, first : first + HEADS * KEY_VALUE_HEADS]
    results = results.reshape(2, N_REQ // 2, DECODE_STEPS, HEADS // 2, KEY_VALUE_HEADS, PAGE)
    results = jnp.transpose(results[::-1], (0, 1, 2, 4, 3, 5))
    decode_output = results.reshape(1, DECODE_SLOTS, DECODE_STEPS, QUERY_HEADS * HEAD_SIZE)
    return (prefill_out, store, decode_output)


def solution(mesh):
    placed = (
        P(("section", "req"), "tp"),
        P(("section", "req"), "tp", None),
        P(("section", "req"), None, "tp", None),
        P(("section", "req"), None),
        P(("section", "req"), "tp", None, None),
        P(),
        P(),
        P(("section", "req"), None, None, None),
        P(("section", "req"), None, None, None, None),
        P(("section", "req"), None, None, None, None),
    )
    return jax.shard_map(
        shards,
        mesh=mesh,
        in_specs=placed,
        out_specs=(
            P(("section", "req"), "tp"),
            P(("section", "req"), None, "tp", None, None, None),
            P(("section", "req"), None, None, None),
        ),
        check_vma=False,
    )
```
